128 devices in a mesh: dp: 4 (over y_lo, core), row: 16 (over x, z), col: 2 (over y_hi).
Axes of the slice: x: 4, y: 4 (y_hi: 2, y_lo: 2; y = y_hi * 2 + y_lo), z: 4, core: 2. Of those that a mesh axis runs over, the one named last changes fastest.
Arguments:
- tokens: bfloat16 [8192, 2048], P(('dp', 'row'), 'col'), may hold values from -6 to 6
- w_heads: bfloat16 [2048, 3, 2048], P('col', None, 'row'), may hold values from -0.125 to 0.125
- query_scale: float32 [2048], P('row'), may hold values from 0.1 to 1.9
- key_scale: float32 [2048], P('row'), may hold values from 0.1 to 1.9
- w_merge: bfloat16 [2048, 2048], P('row', 'col'), may hold values from -0.125 to 0.125
- attend_scale: float32 [2048], P('col'), may hold values from 0.1 to 1.9
- w_gateup: bfloat16 [2048, 2, 8192], P('col', None, 'row'), may hold values from -0.125 to 0.125
- w_down: bfloat16 [8192, 2048], P('row', 'col'), may hold values from -0.0625 to 0.0625
- dense_scale: float32 [2048], P('col'), may hold values from 0.1 to 1.9
- cotangent: bfloat16 [8192, 2048], P(('dp', 'row'), 'col'), may hold values from -6 to 6
Outputs:
- output: bfloat16 [8192, 2048], P(('dp', 'row'), 'col')
- grad_tokens: bfloat16 [8192, 2048], P(('dp', 'row'), 'col')
- grad_heads: float32 [2048, 3, 2048], P('col', None, 'row')
- grad_merge: float32 [2048, 2048], P('row', 'col')
- grad_gateup: float32 [2048, 2, 8192], P('col', None, 'row')
- grad_down: float32 [8192, 2048], P('row', 'col')
- grad_query: float32 [2048], replicated
- grad_key: float32 [2048], replicated
- grad_attend: float32 [2048], replicated
- grad_dense: float32 [2048], replicated
The draws below stay inside these ranges and needn't reach their ends.
All inputs are finite; a program needn't handle non-finite values.
Results may differ from the reference program's by a relative error of at most 0.028.
Values may be sent and summed in bfloat16 or wider, within the bound.
No kernel may reach another device: no remote copies, remote signals or barrier semaphores. Data moves between devices by JAX's collectives and lax.ppermute only.
A program may use at most 128 MiB of HBM per device.

```python
import jax
import jax.numpy as jnp
from jax import lax

D = 2048
F = 8192
HEADS = 16
HEAD_DIM = 128
SEQ_LEN = 1024
TOKENS = 8192


def shard_levels(own_key, dims, pieces, smallest, top_value):
    level = 1.0
    for axis_at, blocks in pieces:
        draws = jax.random.uniform(jax.random.fold_in(jax.random.fold_in(own_key, 6), axis_at), (blocks,), jnp.float32, smallest / len(pieces), top_value / len(pieces))
        level = level * jnp.repeat(jnp.exp(draws), dims[axis_at] // blocks).reshape((-1,) + (1,) * (len(dims) - 1 - axis_at))
    return level


def noise(own_key, dims, scale, most, cuts=(), held_as=jnp.bfloat16):
    values = jax.random.normal(own_key, dims, jnp.float32) * scale
    if len(cuts) > 0:
        values = shard_levels(own_key, dims, cuts, -0.22, 0.18) * values
    return jnp.clip(values, min=-most, max=most).astype(held_as)


def setup_inputs(seed: int = 0) -> dict:
    splits = jax.random.split(jax.random.key(seed), 11)
    tokens = noise(splits[0], (TOKENS, D), 1.0, 6.0, ((0, 64), (1, 2)))
    w_heads = noise(splits[1], (D, 3, D), D ** -0.5, 0.125, ((0, 2), (2, 16)))
    query_scale = jnp.clip(1.0 + 0.18 * jax.random.normal(splits[2], (D,), jnp.float32), 0.1, 1.9)
    key_scale = jnp.clip(1.0 + 0.18 * jax.random.normal(splits[3], (D,), jnp.float32), 0.1, 1.9)
    w_merge = noise(splits[4], (D, D), D ** -0.5, 0.125, ((0, 16), (1, 2)))
    attend_scale = jnp.clip(1.0 + 0.18 * jax.random.normal(splits[5], (D,), jnp.float32), 0.1, 1.9)
    w_gateup = noise(splits[6], (D, 2, F), D ** -0.5, 0.125, ((0, 2), (2, 16)))
    w_down = noise(splits[7], (F, D), F ** -0.5, 0.0625, ((0, 16), (1, 2)))
    dense_scale = jnp.clip(1.0 + 0.18 * jax.random.normal(splits[8], (D,), jnp.float32), 0.1, 1.9)
    cotangent = noise(splits[9], (TOKENS, D), 1.0, 6.0, ((0, 64), (1, 2)))
    return dict(tokens=tokens, w_heads=w_heads, query_scale=query_scale, key_scale=key_scale, w_merge=w_merge, attend_scale=attend_scale, w_gateup=w_gateup, w_down=w_down, dense_scale=dense_scale, cotangent=cotangent)


EPSILON = 1e-06
THETA = 500000.0
NEGATIVE = -1e+30
HIGHEST = lax.Precision.HIGHEST

@jax.custom_vjp
def low(v):
    return lax.optimization_barrier(v.astype(jnp.bfloat16)).astype(jnp.float32)

@jax.custom_vjp
def low_back(v):
    return v

def low_keep(v):
    return (low(v), None)

def low_pass(kept, grad):
    return (grad,)

def back_keep(v):
    return (v, None)

def back_low(kept, grad):
    return (low(grad),)
low.defvjp(low_keep, low_pass)
low_back.defvjp(back_keep, back_low)

def product(left, right):
    return jnp.dot(left, right, precision=HIGHEST, preferred_element_type=jnp.float32)

def normalize(values, scale):
    rate = lax.rsqrt(lax.optimization_barrier(jnp.mean(values * values, axis=-1, keepdims=True)) + EPSILON)
    return values * rate * scale

def rope_tables(place):
    pairs = HEAD_DIM // 2
    freq = THETA ** (-(jnp.arange(pairs, dtype=jnp.float32) * (2.0 / HEAD_DIM)))
    angle = place.astype(jnp.float32)[:, None] * freq[None, :]
    cosine = jnp.concatenate([jnp.cos(angle), jnp.cos(angle)], axis=1)
    sine = jnp.concatenate([jnp.sin(angle), jnp.sin(angle)], axis=1)
    return (cosine[:, None, :], sine[:, None, :])

def rotate(values, cosine, sine):
    pairs = values.shape[-1] // 2
    turned = jnp.concatenate([-values[..., pairs:], values[..., :pairs]], axis=-1)
    return values * cosine + turned * sine

def sequence_forward(seq_tokens, params):
    w_heads, query_scale, key_scale, w_merge, attend_scale, w_gateup, w_down, dense_scale = params
    length = seq_tokens.shape[0]
    scale = HEAD_DIM ** (-0.5)
    projected = low_back(product(seq_tokens, w_heads.reshape(D, 3 * D))).reshape(length, 3, D)
    query = normalize(projected[:, 0], query_scale).reshape(length, HEADS, HEAD_DIM)
    key = normalize(projected[:, 1], key_scale).reshape(length, HEADS, HEAD_DIM)
    place = jnp.arange(length, dtype=jnp.int32)
    cosine, sine = rope_tables(place)
    query_low = low(rotate(query, cosine, sine))
    key_low = low(rotate(key, cosine, sine))
    value_low = low(projected[:, 2].reshape(length, HEADS, HEAD_DIM))
    raw = low_back(jnp.einsum('qhd,khd->hqk', query_low, key_low, precision=HIGHEST, preferred_element_type=jnp.float32) * scale)
    allowed = place[None, :] <= place[:, None]
    masked = jnp.where(allowed[None], raw, NEGATIVE)
    probs = low(jax.nn.softmax(masked, axis=-1))
    mixed = jnp.einsum('hqk,khd->qhd', probs, value_low, precision=HIGHEST, preferred_element_type=jnp.float32)
    mixed = low(low_back(mixed.reshape(length, D)))
    attended = low_back(product(mixed, w_merge))
    hidden = seq_tokens + normalize(attended, attend_scale)
    hidden_low = low(hidden)
    gateup = low_back(product(hidden_low, w_gateup.reshape(D, 2 * F))).reshape(length, 2, F)
    activated = low(jax.nn.silu(gateup[:, 0]) * gateup[:, 1])
    dense = low_back(product(activated, w_down))
    return hidden + normalize(dense, dense_scale)

def reference(tokens, w_heads, query_scale, key_scale, w_merge, attend_scale, w_gateup, w_down, dense_scale, cotangent):
    count = TOKENS // SEQ_LEN
    params = (w_heads.astype(jnp.float32), query_scale, key_scale, w_merge.astype(jnp.float32), attend_scale, w_gateup.astype(jnp.float32), w_down.astype(jnp.float32), dense_scale)
    inputs = tokens.astype(jnp.float32).reshape(count, SEQ_LEN, D)
    cotangents = cotangent.astype(jnp.float32).reshape(count, SEQ_LEN, D)

    def step(totals, pair):
        result, pullback = jax.vjp(sequence_forward, pair[0], params)
        tokens_back, params_back = pullback(pair[1])
        return (jax.tree.map(jnp.add, totals, params_back), (result, tokens_back))
    zeros = jax.tree.map(jnp.zeros_like, params)
    totals, (results, backs) = lax.scan(step, zeros, (inputs, cotangents))
    return (results.reshape(TOKENS, D).astype(jnp.bfloat16), backs.reshape(TOKENS, D).astype(jnp.bfloat16), totals[0], totals[3], totals[5], totals[6], totals[1], totals[2], totals[4], totals[7])
```

```python
import itertools

import jax
import jax.numpy as jnp
from jax import lax
from jax.sharding import Mesh
from jax.sharding import PartitionSpec as P

D = 2048
HEAD_DIM = 128
SEQ_LEN = 1024
HALF = 1024
SUB = 64
EPSILON = 1e-06
THETA = 500000.0
NEGATIVE = -1e30

LOW = jnp.bfloat16
WIDE = jnp.float32

NAMES = ("yl", "core", "xh", "xl", "z", "yh")
SIZES = {"yl": 2, "core": 2, "xh": 2, "xl": 2, "z": 4, "yh": 2}


def contract(left, right, left_dim, right_dim):
    return lax.dot_general(
        left, right, (((left_dim,), (right_dim,)), ((), ())), preferred_element_type=WIDE
    )


def pairs_of(axes, target):
    sizes = [SIZES[name] for name in axes]

    def flat(place):
        index = 0
        for value, size in zip(place, sizes):
            index = index * size + value
        return index

    return [
        (flat(place), flat(target(*place)))
        for place in itertools.product(*[range(size) for size in sizes])
    ]


def move(value, axes, target):
    return lax.ppermute(value, axes, pairs_of(axes, target))


def to_core(value):
    return move(value, ("core",), lambda c: (1 - c,))


def to_sibling(value):
    return move(value, ("yl",), lambda a: (1 - a,))


def slice_near(value):
    return move(
        value,
        ("core", "xh", "xl"),
        lambda c, a, b: (c, 1 - a, 1 - b) if c == a else (1 - c, a, b),
    )


def give_near(value):
    return move(
        value,
        ("core", "xh", "xl"),
        lambda c, a, b: (1 - c, a, b) if c == a else (c, 1 - a, 1 - b),
    )


def slice_far(value):
    return move(
        value,
        ("yl", "core", "xh", "xl", "yh"),
        lambda l, c, a, b, h: (1 - l, c, a, b, 1 - h)
        if c == a
        else (1 - l, 1 - c, 1 - a, 1 - b, 1 - h),
    )


def beside(function, value, rides, work=()):
    value, arrays = lax.optimization_barrier((value, tuple(array for _, array in rides)))
    moved = tuple(ride(array) for (ride, _), array in zip(rides, arrays))
    return lax.optimization_barrier((function(value), moved, work))


def exchange(rows):
    return lax.all_to_all(rows, ("xl", "z"), 0, 0, tiled=True)


def gather_tokens(shard, function, rides=(), work=()):
    copies = jnp.broadcast_to(shard[None], (8,) + shard.shape).reshape(8 * SUB, shard.shape[1])
    own, moved, work = beside(exchange, copies, rides, work)
    first, other = lax.optimization_barrier((function(0, own), to_core(own)))
    return (own, other), (first, function(1, other)), moved, work


def scatter_tokens(function, rides=(), work=()):
    arrived = to_core(function(1).astype(LOW))
    own, arrived = lax.optimization_barrier((function(0).astype(LOW), arrived))
    arrived, moved, work = beside(exchange, add_low(own, arrived), rides, work)
    total = jnp.sum(arrived.reshape(8, SUB, arrived.shape[1]).astype(WIDE), axis=0)
    return total, moved, work


def by_core(first, second):
    own_first = lax.axis_index("core") == 0
    return jnp.where(own_first, first, second), jnp.where(own_first, second, first)


def group_copies(rows):
    copies = jnp.broadcast_to(rows[None], (16,) + rows.shape).reshape(-1, 128)
    arrived = lax.all_to_all(copies, ("core", "xl", "z"), 0, 0, tiled=True)
    return arrived.reshape((16,) + rows.shape)


def group_sums(own, other, more=None):
    whole = jnp.concatenate(by_core(own, other), axis=0).reshape(16, 128)
    if more is not None:
        whole = jnp.concatenate([whole, more], axis=0)
    arrived = group_copies(whole)
    total = jnp.sum(arrived[:, :16], axis=0).reshape(2, 2, 512)
    return by_core(total[0], total[1]), arrived[:, 16:]


def other_groups(rows):
    axes = ("yl", "xh", "yh")
    copies = jnp.broadcast_to(rows[None], (8,) + rows.shape).reshape(-1, 128)
    arrived = lax.all_to_all(copies, axes, 0, 0, tiled=True)
    return jnp.sum(arrived.reshape((8,) + rows.shape), axis=0)


def both(function, *pairs):
    return tuple(function(*items) for items in zip(*pairs))


def add_low(first, *others):
    total = first.astype(WIDE)
    for other in others:
        total = total + other.astype(WIDE)
    return total.astype(LOW)


def regroup(block):
    core = lax.axis_index("core")
    high = lax.axis_index("yh")
    lower, upper = block[:SUB], block[SUB:]
    parts = []
    for j in (0, 1):
        piece = jnp.where((high ^ j) == 0, lower, upper)
        parts.append(move(piece, ("core", "yh"), lambda c, h: (h ^ j, c)))
    same = core == high
    return jnp.concatenate(
        [jnp.where(same, parts[0], parts[1]), jnp.where(same, parts[1], parts[0])], axis=1
    )


def ungroup(block):
    core = lax.axis_index("core")
    high = lax.axis_index("yh")
    near, far = block[:, :HALF], block[:, HALF:]
    parts = []
    for j in (0, 1):
        piece = jnp.where((core ^ j) == high, near, far)
        parts.append(move(piece, ("core", "yh"), lambda c, h: (h, c ^ j)))
    first = high == 0
    return jnp.concatenate(
        [jnp.where(first, parts[0], parts[1]), jnp.where(first, parts[1], parts[0])], axis=0
    )


def half_of_both(arrived_near, arrived_far):
    part = arrived_near.astype(WIDE) + arrived_far.astype(WIDE)
    rows = part.shape[0] // 2
    core = lax.axis_index("core")
    lower, upper = part[:rows], part[rows:]
    keep = jnp.where(core == 0, lower, upper)
    give = jnp.where(core == 0, upper, lower).astype(LOW)
    return (keep + to_core(give).astype(WIDE)).astype(LOW)


def whole_of_half(half, arrived):
    core = lax.axis_index("core")
    half = add_low(half, arrived)
    other = to_core(half)
    return jnp.concatenate(
        [jnp.where(core == 0, half, other), jnp.where(core == 0, other, half)], axis=0
    ).astype(WIDE)


def rope_tables(place):
    pairs = HEAD_DIM // 2
    freq = THETA ** (-(jnp.arange(pairs, dtype=WIDE) * (2.0 / HEAD_DIM)))
    angle = place.astype(WIDE)[:, None] * freq[None, :]
    cosine = jnp.concatenate([jnp.cos(angle), jnp.cos(angle)], axis=1)
    sine = jnp.concatenate([jnp.sin(angle), jnp.sin(angle)], axis=1)
    return (cosine, sine)


def rotate(values, cosine, sine):
    pairs = HEAD_DIM // 2
    turned = jnp.concatenate([-values[:, pairs:], values[:, :pairs]], axis=1)
    return values * cosine + turned * sine


def rotate_back(grad, cosine, sine):
    pairs = HEAD_DIM // 2
    scaled = grad * sine
    turned = jnp.concatenate([scaled[:, pairs:], -scaled[:, :pairs]], axis=1)
    return grad * cosine + turned


def local(
    tokens,
    w_heads,
    query_scale,
    key_scale,
    w_merge,
    attend_scale,
    w_gateup,
    w_down,
    dense_scale,
    cotangent,
):
    core = lax.axis_index("core")
    xh = lax.axis_index("xh")
    xl = lax.axis_index("xl")
    z = lax.axis_index("z")
    high = lax.axis_index("yh")

    shard = regroup(tokens)
    heads_in = w_heads.reshape(HALF, 3 * HEAD_DIM)
    gateup_in = lax.optimization_barrier(w_gateup.reshape(HALF, 2 * 512))
    head_scales = slice_near(jnp.stack([query_scale, key_scale]))
    query_scale, key_scale = head_scales[0], head_scales[1]
    width_scales = jnp.stack([attend_scale, dense_scale])
    width_scales = jnp.concatenate(
        [
            width_scales,
            move(width_scales, ("yl", "yh"), lambda l, h: (1 - l, 1 - h)),
        ],
        axis=1,
    )
    attend_scale, dense_scale = width_scales[0], width_scales[1]
    grad_out = regroup(cotangent)

    index = jnp.arange(512, dtype=jnp.int32)
    place = index // SUB * 128 + index % SUB
    places = (place + core * SUB, place + (1 - core) * SUB)
    key_place = jnp.concatenate(places)
    tables = both(rope_tables, places)
    scale = HEAD_DIM ** (-0.5)

    copies = jnp.broadcast_to(shard[None], (8,) + shard.shape).reshape(8 * SUB, D)
    own, moved, (tables, grad_out, gateup_in) = beside(
        exchange,
        copies,
        (
            (slice_near, heads_in),
            (slice_far, heads_in),
            (slice_near, w_merge),
            (slice_far, w_merge),
        ),
        (tables, grad_out, gateup_in),
    )
    grad_out = grad_out.astype(WIDE)
    heads = jnp.concatenate(moved[:2], axis=0)
    merge = jnp.concatenate(moved[2:], axis=1)

    def squares(query, key):
        return jnp.stack([jnp.sum(query * query, axis=1), jnp.sum(key * key, axis=1)])

    def attend_whole(own):
        first, other = lax.optimization_barrier((contract(own, heads, 1, 0), to_core(own)))
        projected = (first, contract(other, heads, 1, 0))
        query_raw = both(lambda rows: rows[:, :HEAD_DIM], projected)
        key_raw = both(lambda rows: rows[:, HEAD_DIM : 2 * HEAD_DIM], projected)
        value_low = jnp.concatenate(
            both(lambda rows: rows[:, 2 * HEAD_DIM :].astype(LOW), projected), axis=0
        )
        powers, _ = group_sums(*both(squares, query_raw, key_raw))
        rates = both(lambda rows: lax.rsqrt(rows / D + EPSILON), powers)
        query_rate = both(lambda rows: rows[0][:, None], rates)
        key_rate = both(lambda rows: rows[1][:, None], rates)
        query_hat = both(lambda raw, rate: raw * rate, query_raw, query_rate)
        key_hat = both(lambda raw, rate: raw * rate, key_raw, key_rate)
        query_low = both(
            lambda hat, table: rotate(hat * query_scale, *table).astype(LOW), query_hat, tables
        )
        key_low = jnp.concatenate(
            both(lambda hat, table: rotate(hat * key_scale, *table).astype(LOW), key_hat, tables),
            axis=0,
        )

        def attend(query, place):
            scores = scores_of(query, key_low, place)
            top = jnp.max(scores, axis=1, keepdims=True)
            shifted = jnp.exp(scores - top)
            total = jnp.sum(shifted, axis=1, keepdims=True)
            probs_low = (shifted / total).astype(LOW)
            mixed = contract(probs_low, value_low, 1, 0).astype(LOW)
            return mixed, top + jnp.log(total)

        attention = both(attend, query_low, places)
        mixed_low = both(lambda pair: pair[0], attention)
        log_total = both(lambda pair: pair[1], attention)
        return (
            (own, other),
            (query_rate, key_rate, query_hat, key_hat),
            (query_low, key_low, value_low),
            mixed_low,
            log_total,
        )

    def scores_of(query, key_low, place):
        allowed = key_place[None, :] <= place[:, None]
        return jnp.where(allowed, contract(query, key_low, 1, 1) * scale, NEGATIVE)

    (whole, norms, lows, mixed_low, log_total), gateup_parts, _ = beside(
        attend_whole, own, ((slice_near, gateup_in), (slice_far, gateup_in))
    )
    query_rate, key_rate, query_hat, key_hat = norms
    query_low, key_low, value_low = lows
    gateup_w = jnp.concatenate(gateup_parts, axis=0)

    attended, down_parts, gateup_w = scatter_tokens(
        lambda i: contract(mixed_low[i], merge, 1, 0),
        ((slice_near, w_down), (slice_far, w_down)),
        gateup_w,
    )
    attend_rate = lax.rsqrt(jnp.mean(attended * attended, axis=1, keepdims=True) + EPSILON)
    attend_hat = attended * attend_rate
    hidden = shard.astype(WIDE) + attend_hat * attend_scale

    def feed(i, rows):
        gateup = contract(rows, gateup_w, 1, 0)
        gate, upper = gateup[:, :512], gateup[:, 512:]
        return gate, upper, (gate * jax.nn.sigmoid(gate) * upper).astype(LOW)

    hidden_whole, fed, _, down = gather_tokens(
        hidden.astype(LOW), feed, (), jnp.concatenate(down_parts, axis=1)
    )
    act_low = both(lambda parts: parts[2], fed)
    dense, _, _ = scatter_tokens(lambda i: contract(act_low[i], down, 1, 0))
    dense_rate = lax.rsqrt(jnp.mean(dense * dense, axis=1, keepdims=True) + EPSILON)
    dense_hat = dense * dense_rate
    output = (hidden + dense_hat * dense_scale).astype(LOW)

    dense_scaled = grad_out * dense_scale
    dense_dot = jnp.mean(dense_scaled * dense_hat, axis=1, keepdims=True)
    dense_back_low = (dense_rate * (dense_scaled - dense_hat * dense_dot)).astype(LOW)
    dense_part = jnp.sum(grad_out * dense_hat, axis=0)

    def back_through(i, rows):
        gate, upper, _ = fed[i]
        act_back = contract(rows, down, 1, 1)
        sigmoid = jax.nn.sigmoid(gate)
        gate_back = act_back * upper * sigmoid * (1.0 + gate * (1.0 - sigmoid))
        up_back = act_back * (gate * sigmoid)
        return jnp.concatenate([gate_back, up_back], axis=1).astype(LOW)

    dense_back, gateup_back_low, _, _ = gather_tokens(dense_back_low, back_through)

    def weight_grad(left, right):
        return (contract(left[0], right[0], 0, 0) + contract(left[1], right[1], 0, 0)).astype(LOW)

    grad_down = weight_grad(act_low, dense_back)
    hidden_back, down_parts, (grad_gateup, output) = scatter_tokens(
        lambda i: contract(gateup_back_low[i], gateup_w, 1, 1),
        ((give_near, grad_down[:, :HALF]), (slice_far, grad_down[:, HALF:])),
        (weight_grad(hidden_whole, gateup_back_low), ungroup(output)),
    )
    hidden_back = grad_out + hidden_back

    attend_scaled = hidden_back * attend_scale
    attend_dot = jnp.mean(attend_scaled * attend_hat, axis=1, keepdims=True)
    attended_back_low = (attend_rate * (attend_scaled - attend_hat * attend_dot)).astype(LOW)
    attend_part = jnp.sum(hidden_back * attend_hat, axis=0)

    attended_back, mixed_back_low, gateup_upper, _ = gather_tokens(
        attended_back_low,
        lambda i, rows: contract(rows, merge, 1, 1).astype(LOW),
        ((give_near, grad_gateup[:512]), (slice_far, grad_gateup[HALF : HALF + 512])),
    )
    grad_merge = weight_grad(mixed_low, attended_back)
    down_half = half_of_both(*down_parts)
    gateup_upper = half_of_both(*gateup_upper)

    def attend_back(query, place, log_total, mixed_back):
        probs = jnp.exp(scores_of(query, key_low, place) - log_total)
        probs_back = contract(mixed_back, value_low, 1, 1)
        row_dot = jnp.sum(probs_back * probs, axis=1, keepdims=True)
        scores_back = (probs * (probs_back - row_dot)).astype(LOW)
        query_turned = contract(scores_back, key_low, 1, 0) * scale
        return query_turned, scores_back, probs.astype(LOW)

    def products(query, query_hat, key, key_hat):
        return jnp.stack([jnp.sum(query * query_hat, axis=1), jnp.sum(key * key_hat, axis=1)])

    def through_norm(rate, scaled, hat, dot):
        return rate * (scaled - hat * dot[:, None])

    def column_sum(first, second):
        return sum(both(lambda a, b: jnp.sum(a * b, axis=0), first, second))

    def attend_whole_back(mixed_back_low):
        backs = both(attend_back, query_low, places, log_total, mixed_back_low)
        query_norm_back = both(lambda back, table: rotate_back(back[0], *table), backs, tables)
        scores_back = (backs[0][1], backs[1][1])
        probs_low = (backs[0][2], backs[1][2])
        key_turned = scale * (
            contract(scores_back[0], query_low[0], 0, 0)
            + contract(scores_back[1], query_low[1], 0, 0)
        )
        value_back = contract(probs_low[0], mixed_back_low[0], 0, 0) + contract(
            probs_low[1], mixed_back_low[1], 0, 0
        )
        value_back = (value_back[:512], value_back[512:])
        key_norm_back = both(
            lambda rows, table: rotate_back(rows, *table),
            (key_turned[:512], key_turned[512:]),
            tables,
        )
        query_scaled = both(lambda rows: rows * query_scale, query_norm_back)
        key_scaled = both(lambda rows: rows * key_scale, key_norm_back)
        parts = jnp.concatenate(
            [
                column_sum(query_norm_back, query_hat)[None],
                column_sum(key_norm_back, key_hat)[None],
                attend_part.reshape(16, 128),
                dense_part.reshape(16, 128),
            ],
            axis=0,
        )
        dots, parts = group_sums(
            *both(products, query_scaled, query_hat, key_scaled, key_hat), parts
        )
        query_back = both(
            through_norm, query_rate, query_scaled, query_hat, (dots[0][0] / D, dots[1][0] / D)
        )
        key_back = both(
            through_norm, key_rate, key_scaled, key_hat, (dots[0][1] / D, dots[1][1] / D)
        )
        back = both(
            lambda *parts: jnp.concatenate(parts, axis=1).astype(LOW),
            query_back,
            key_back,
            value_back,
        )
        return back, parts

    (projected_back_low, parts), moved, _ = beside(
        attend_whole_back,
        mixed_back_low,
        (
            (give_near, grad_gateup[512:HALF]),
            (slice_far, grad_gateup[HALF + 512 :]),
            (give_near, grad_merge[:, :HALF]),
            (slice_far, grad_merge[:, HALF:]),
            (to_sibling, down_half),
        ),
    )
    gateup_lower = half_of_both(*moved[:2])
    merge_half = half_of_both(*moved[2:4])
    grad_heads = weight_grad(whole, projected_back_low)

    rows = parts[:, :2].reshape(2, 2, 4, 2, 128)
    straight = (jnp.arange(2) == xh)[:, None, None, None, None]
    rows = jnp.where(straight, rows, rows[:, ::-1])
    rows = jnp.moveaxis(rows.reshape(16, 2, 128), 1, 0).reshape(32, 128)
    width = jnp.sum(parts[:, 2:], axis=0).reshape(2, 2, 8, 128)
    width = jnp.where(high == 0, width, width[:, ::-1]).reshape(32, 128)
    gains = jnp.concatenate([rows, width], axis=0)

    tokens_back, moved, grad_down = scatter_tokens(
        lambda i: contract(projected_back_low[i], heads, 1, 1),
        (
            (give_near, grad_heads[:HALF]),
            (slice_far, grad_heads[HALF:]),
            (to_sibling, gateup_upper),
            (to_sibling, gateup_lower),
            (to_sibling, merge_half),
            (other_groups, gains),
        ),
        whole_of_half(down_half, moved[4]),
    )
    grad_tokens = ungroup((hidden_back + tokens_back).astype(LOW))
    heads_half = half_of_both(*moved[:2])
    grad_heads = whole_of_half(heads_half, to_sibling(heads_half))
    grad_gateup = jnp.concatenate(
        [whole_of_half(gateup_upper, moved[2]), whole_of_half(gateup_lower, moved[3])], axis=0
    )
    grad_merge = whole_of_half(merge_half, moved[4])
    gains = moved[5].reshape(4, D)
    return (
        output,
        grad_tokens,
        grad_heads.reshape(HALF, 3, HEAD_DIM),
        grad_merge,
        grad_gateup.reshape(HALF, 2, 512),
        grad_down,
        gains[0],
        gains[1],
        gains[2],
        gains[3],
    )


def solution(mesh):
    fine = Mesh(mesh.devices.reshape(tuple(SIZES[name] for name in NAMES)), NAMES)
    dp, row, col = ("yl", "core"), ("xh", "xl", "z"), "yh"
    in_specs = (
        P(dp + row, col),
        P(col, None, row),
        P(row),
        P(row),
        P(row, col),
        P(col),
        P(col, None, row),
        P(row, col),
        P(col),
        P(dp + row, col),
    )
    out_specs = (
        P(dp + row, col),
        P(dp + row, col),
        P(col, None, row),
        P(row, col),
        P(col, None, row),
        P(row, col),
        P(),
        P(),
        P(),
        P(),
    )
    return jax.shard_map(local, mesh=fine, in_specs=in_specs, out_specs=out_specs, check_vma=False)
```

```python
import itertools

import jax
import jax.numpy as jnp
from jax import lax
from jax.experimental import pallas as pl
from jax.experimental.pallas import tpu as pltpu
from jax.sharding import Mesh
from jax.sharding import PartitionSpec as P

D = 2048
HEAD_DIM = 128
SEQ_LEN = 1024
HALF = 1024
SUB = 64
EPSILON = 1e-06
THETA = 500000.0
NEGATIVE = -1e30

LOW = jnp.bfloat16
WIDE = jnp.float32

NAMES = ("yl", "core", "xh", "xl", "z", "yh")
SIZES = {"yl": 2, "core": 2, "xh": 2, "xl": 2, "z": 4, "yh": 2}


def contract(left, right, left_dim, right_dim):
    return lax.dot_general(
        left, right, (((left_dim,), (right_dim,)), ((), ())), preferred_element_type=WIDE
    )


def pairs_of(axes, target):
    sizes = [SIZES[name] for name in axes]

    def flat(place):
        index = 0
        for value, size in zip(place, sizes):
            index = index * size + value
        return index

    return [
        (flat(place), flat(target(*place)))
        for place in itertools.product(*[range(size) for size in sizes])
    ]


def move(value, axes, target):
    return lax.ppermute(value, axes, pairs_of(axes, target))


def to_core(value):
    return move(value, ("core",), lambda c: (1 - c,))


def to_sibling(value):
    return move(value, ("yl",), lambda a: (1 - a,))


def slice_near(value):
    return move(
        value,
        ("core", "xh", "xl"),
        lambda c, a, b: (c, 1 - a, 1 - b) if c == a else (1 - c, a, b),
    )


def give_near(value):
    return move(
        value,
        ("core", "xh", "xl"),
        lambda c, a, b: (1 - c, a, b) if c == a else (c, 1 - a, 1 - b),
    )


def slice_far(value):
    return move(
        value,
        ("yl", "core", "xh", "xl", "yh"),
        lambda l, c, a, b, h: (1 - l, c, a, b, 1 - h)
        if c == a
        else (1 - l, 1 - c, 1 - a, 1 - b, 1 - h),
    )


def after(value, arrays):
    return lax.optimization_barrier((value, arrays))[1]


def beside(function, value, rides, work=()):
    value, arrays = lax.optimization_barrier((value, tuple(array for _, array in rides)))
    moved = tuple(ride(array) for (ride, _), array in zip(rides, arrays))
    return lax.optimization_barrier((function(value), moved, work))


def exchange(rows):
    return lax.all_to_all(rows, ("xl", "z"), 0, 0, tiled=True)


def gather_tokens(shard, function, rides=(), work=()):
    copies = jnp.broadcast_to(shard[None], (8,) + shard.shape).reshape(8 * SUB, shard.shape[1])
    own, moved, work = beside(exchange, copies, rides, work)
    first, other = lax.optimization_barrier((function(0, own), to_core(own)))
    return (own, other), (first, function(1, other)), moved, work


def scatter_tokens(function, rides=(), work=()):
    arrived = to_core(function(1).astype(LOW))
    own, arrived = lax.optimization_barrier((function(0).astype(LOW), arrived))
    arrived, moved, work = beside(exchange, add_low(own, arrived), rides, work)
    total = jnp.sum(arrived.reshape(8, SUB, arrived.shape[1]).astype(WIDE), axis=0)
    return total, moved, work


def by_core(first, second):
    own_first = lax.axis_index("core") == 0
    return jnp.where(own_first, first, second), jnp.where(own_first, second, first)


def group_copies(rows):
    copies = jnp.broadcast_to(rows[None], (16,) + rows.shape).reshape(-1, 128)
    arrived = lax.all_to_all(copies, ("core", "xl", "z"), 0, 0, tiled=True)
    return arrived.reshape((16,) + rows.shape)


def group_sums(own, other, more=None):
    whole = jnp.concatenate(by_core(own, other), axis=0).reshape(16, 128)
    if more is not None:
        whole = jnp.concatenate([whole, more], axis=0)
    arrived = group_copies(whole)
    total = jnp.sum(arrived[:, :16], axis=0).reshape(2, 2, 512)
    return by_core(total[0], total[1]), arrived[:, 16:]


def by_slice(blocks):
    view = blocks.reshape((2, 2, 4) + blocks.shape[1:])
    straight = jnp.arange(2) == lax.axis_index("xh")
    straight = straight.reshape((2,) + (1,) * (view.ndim - 2))
    first = jnp.where(straight, view[:, 0], view[:, 1])
    second = jnp.where(straight, view[:, 1], view[:, 0])
    return jnp.stack([first, second], axis=1).reshape(blocks.shape)


def to_owners(own, other):
    blocks = jnp.concatenate(by_core(own, other), axis=0)
    arrived = lax.all_to_all(blocks, ("core", "xl", "z"), 0, 0, tiled=True)
    return jnp.swapaxes(arrived.reshape(16, SUB, HEAD_DIM), 0, 1).reshape(SUB, D)


def to_heads(rows):
    blocks = jnp.swapaxes(rows.reshape(SUB, 16, HEAD_DIM), 0, 1).reshape(16 * SUB, HEAD_DIM)
    return lax.all_to_all(blocks, ("core", "xl", "z"), 0, 0, tiled=True)


def both(function, *pairs):
    return tuple(function(*items) for items in zip(*pairs))


def add_low(first, *others):
    total = first.astype(WIDE)
    for other in others:
        total = total + other.astype(WIDE)
    return total.astype(LOW)


def regroup(block):
    core = lax.axis_index("core")
    high = lax.axis_index("yh")
    lower, upper = block[:SUB], block[SUB:]
    parts = []
    for j in (0, 1):
        piece = jnp.where((high ^ j) == 0, lower, upper)
        parts.append(move(piece, ("core", "yh"), lambda c, h: (h ^ j, c)))
    same = core == high
    return jnp.concatenate(
        [jnp.where(same, parts[0], parts[1]), jnp.where(same, parts[1], parts[0])], axis=1
    )


def ungroup(block):
    core = lax.axis_index("core")
    high = lax.axis_index("yh")
    near, far = block[:, :HALF], block[:, HALF:]
    parts = []
    for j in (0, 1):
        piece = jnp.where((core ^ j) == high, near, far)
        parts.append(move(piece, ("core", "yh"), lambda c, h: (h, c ^ j)))
    first = high == 0
    return jnp.concatenate(
        [jnp.where(first, parts[0], parts[1]), jnp.where(first, parts[1], parts[0])], axis=0
    )


def half_of_both(arrived_near, arrived_far):
    part = arrived_near.astype(WIDE) + arrived_far.astype(WIDE)
    rows = part.shape[0] // 2
    core = lax.axis_index("core")
    lower, upper = part[:rows], part[rows:]
    keep = jnp.where(core == 0, lower, upper)
    give = jnp.where(core == 0, upper, lower).astype(LOW)
    return (keep + to_core(give).astype(WIDE)).astype(LOW)


def halves_of_sibling(parts):
    half = half_of_both(*parts)
    return half, to_sibling(half)


def whole_of_half(half, arrived):
    core = lax.axis_index("core")
    half = add_low(half, arrived)
    other = to_core(half)
    return jnp.concatenate(
        [jnp.where(core == 0, half, other), jnp.where(core == 0, other, half)], axis=0
    ).astype(WIDE)


def rope_tables(place):
    pairs = HEAD_DIM // 2
    freq = THETA ** (-(jnp.arange(pairs, dtype=WIDE) * (2.0 / HEAD_DIM)))
    angle = place.astype(WIDE)[:, None] * freq[None, :]
    cosine = jnp.concatenate([jnp.cos(angle), jnp.cos(angle)], axis=1)
    sine = jnp.concatenate([jnp.sin(angle), jnp.sin(angle)], axis=1)
    return (cosine, sine)


def rotate(values, cosine, sine):
    pairs = HEAD_DIM // 2
    turned = jnp.concatenate([-values[:, pairs:], values[:, :pairs]], axis=1)
    return values * cosine + turned * sine


def rotate_back(grad, cosine, sine):
    pairs = HEAD_DIM // 2
    scaled = grad * sine
    turned = jnp.concatenate([scaled[:, pairs:], -scaled[:, :pairs]], axis=1)
    return grad * cosine + turned


ROWS = 256
SCALE = HEAD_DIM ** (-0.5)


def places_of(index, core):
    block, row = (index % 512) // SUB, index % SUB
    return block * 128 + jnp.where(index < 512, core, 1 - core) * SUB + row


def block_scores(core_ref, query, key):
    first = pl.program_id(0) * ROWS
    query_index = first + lax.broadcasted_iota(jnp.int32, (ROWS, 1), 0)
    key_index = lax.broadcasted_iota(jnp.int32, (1, SEQ_LEN), 1)
    core = core_ref[0]
    allowed = places_of(key_index, core) <= places_of(query_index, core)
    return jnp.where(allowed, contract(query, key, 1, 1) * SCALE, NEGATIVE)


def attend_kernel(core_ref, query_ref, key_ref, value_ref, mixed_ref, total_ref):
    scores = block_scores(core_ref, query_ref[...], key_ref[...])
    top = jnp.max(scores, axis=1, keepdims=True)
    shifted = jnp.exp(scores - top)
    total = jnp.sum(shifted, axis=1, keepdims=True)
    probs_low = (shifted * (1.0 / total)).astype(LOW)
    mixed_ref[...] = contract(probs_low, value_ref[...], 1, 0).astype(LOW)
    total_ref[...] = jnp.broadcast_to(top + jnp.log(total), total_ref.shape)


def attend_back_kernel(
    core_ref,
    query_ref,
    key_ref,
    value_ref,
    total_ref,
    mixed_back_ref,
    query_out,
    key_out,
    value_out,
):
    query, key, mixed_back = query_ref[...], key_ref[...], mixed_back_ref[...]
    probs = jnp.exp(block_scores(core_ref, query, key) - total_ref[...][:, :1])
    probs_back = contract(mixed_back, value_ref[...], 1, 1)
    row_dot = jnp.sum(probs_back * probs, axis=1, keepdims=True)
    scores_back = (probs * (probs_back - row_dot)).astype(LOW)
    query_out[...] = contract(scores_back, key, 1, 0) * SCALE
    key_part = contract(scores_back, query, 0, 0) * SCALE
    value_part = contract(probs.astype(LOW), mixed_back, 0, 0)

    @pl.when(pl.program_id(0) == 0)
    def _():
        key_out[...] = key_part
        value_out[...] = value_part

    @pl.when(pl.program_id(0) > 0)
    def _():
        key_out[...] += key_part
        value_out[...] += value_part


def row_spec():
    return pl.BlockSpec((ROWS, HEAD_DIM), lambda i: (i, 0))


def whole_spec():
    return pl.BlockSpec((SEQ_LEN, HEAD_DIM), lambda i: (0, 0))


def core_spec():
    return pl.BlockSpec(memory_space=pltpu.SMEM)


def head_call(kernel, in_specs, out_specs, out_types):
    return pl.pallas_call(
        kernel,
        grid=(SEQ_LEN // ROWS,),
        in_specs=in_specs,
        out_specs=out_specs,
        out_shape=[jax.ShapeDtypeStruct((SEQ_LEN, HEAD_DIM), kind) for kind in out_types],
        compiler_params=pltpu.CompilerParams(vmem_limit_bytes=32 * 1024 * 1024),
        cost_estimate=pl.CostEstimate(flops=0, bytes_accessed=0, transcendentals=0),
    )


def attend(core, query, key, value):
    return head_call(
        attend_kernel,
        [core_spec(), row_spec(), whole_spec(), whole_spec()],
        [row_spec(), row_spec()],
        [LOW, WIDE],
    )(core, query, key, value)


def attend_back(core, query, key, value, total, mixed_back):
    return head_call(
        attend_back_kernel,
        [core_spec(), row_spec(), whole_spec(), whole_spec(), row_spec(), row_spec()],
        [row_spec(), whole_spec(), whole_spec()],
        [WIDE, WIDE, WIDE],
    )(core, query, key, value, total, mixed_back)


def local(
    tokens,
    w_heads,
    query_scale,
    key_scale,
    w_merge,
    attend_scale,
    w_gateup,
    w_down,
    dense_scale,
    cotangent,
):
    core = lax.axis_index("core")
    xh = lax.axis_index("xh")
    xl = lax.axis_index("xl")
    z = lax.axis_index("z")
    high = lax.axis_index("yh")

    shard = regroup(tokens)
    heads_in = w_heads.reshape(HALF, 3 * HEAD_DIM)
    gateup_in = w_gateup.reshape(HALF, 2 * 512)
    head_scales = slice_near(jnp.stack([query_scale, key_scale]))
    query_scale, key_scale = head_scales[0], head_scales[1]
    width_scales = jnp.stack([attend_scale, dense_scale])
    width_scales = jnp.concatenate(
        [
            width_scales,
            move(width_scales, ("yl", "yh"), lambda l, h: (1 - l, 1 - h)),
        ],
        axis=1,
    )
    attend_scale, dense_scale = width_scales[0], width_scales[1]
    grad_out = regroup(cotangent)

    index = jnp.arange(512, dtype=jnp.int32)
    place = index // SUB * 128 + index % SUB
    places = (place + core * SUB, place + (1 - core) * SUB)
    tables = both(rope_tables, places)
    core_in = core.astype(jnp.int32)[None]

    copies = jnp.broadcast_to(shard[None], (8,) + shard.shape).reshape(8 * SUB, D)
    merge_in = after(copies, w_merge)
    merge_parts = (slice_near(merge_in), slice_far(merge_in))
    own, moved, (tables, grad_out, gateup_in, merge) = beside(
        exchange,
        copies,
        (
            (slice_near, heads_in),
            (slice_far, heads_in),
        ),
        (tables, grad_out, gateup_in, jnp.concatenate(merge_parts, axis=1)),
    )
    grad_out = grad_out.astype(WIDE)
    heads = jnp.concatenate(moved, axis=0)
    merge = lax.all_gather(merge, ("core", "xl", "z"), axis=0, tiled=True)

    def squares(query, key):
        return jnp.stack([jnp.sum(query * query, axis=1), jnp.sum(key * key, axis=1)])

    def attend_whole(own):
        first, other = lax.optimization_barrier((contract(own, heads, 1, 0), to_core(own)))
        projected = (first, contract(other, heads, 1, 0))
        query_raw = both(lambda rows: rows[:, :HEAD_DIM], projected)
        key_raw = both(lambda rows: rows[:, HEAD_DIM : 2 * HEAD_DIM], projected)
        value_low = jnp.concatenate(
            both(lambda rows: rows[:, 2 * HEAD_DIM :].astype(LOW), projected), axis=0
        )
        powers, _ = group_sums(*both(squares, query_raw, key_raw))
        rates = both(lambda rows: lax.rsqrt(rows / D + EPSILON), powers)
        query_rate = both(lambda rows: rows[0][:, None], rates)
        key_rate = both(lambda rows: rows[1][:, None], rates)
        query_hat = both(lambda raw, rate: raw * rate, query_raw, query_rate)
        key_hat = both(lambda raw, rate: raw * rate, key_raw, key_rate)
        query_low = jnp.concatenate(
            both(
                lambda hat, table: rotate(hat * query_scale, *table).astype(LOW), query_hat, tables
            ),
            axis=0,
        )
        key_low = jnp.concatenate(
            both(lambda hat, table: rotate(hat * key_scale, *table).astype(LOW), key_hat, tables),
            axis=0,
        )

        mixed_low, log_total = attend(core_in, query_low, key_low, value_low)
        attended = contract(to_owners(mixed_low[:512], mixed_low[512:]), merge, 1, 0)
        return (
            (own, other),
            (query_rate, key_rate, query_hat, key_hat),
            (query_low, key_low, value_low),
            mixed_low,
            log_total,
            attended,
        )

    (whole, norms, lows, mixed_low, log_total, attended), gateup_parts, _ = beside(
        attend_whole, own, ((slice_near, gateup_in), (slice_far, gateup_in))
    )
    query_rate, key_rate, query_hat, key_hat = norms
    query_low, key_low, value_low = lows
    attend_rate = lax.rsqrt(jnp.mean(attended * attended, axis=1, keepdims=True) + EPSILON)
    attend_hat = attended * attend_rate
    hidden = shard.astype(WIDE) + attend_hat * attend_scale

    copies = jnp.broadcast_to(hidden.astype(LOW)[None], (8, SUB, D)).reshape(8 * SUB, D)
    own, down_parts, gateup_w = beside(
        exchange,
        copies,
        ((slice_near, w_down), (slice_far, w_down)),
        jnp.concatenate(gateup_parts, axis=0),
    )

    def feed(rows):
        gateup = contract(rows, gateup_w, 1, 0)
        gate, upper = gateup[:, :512], gateup[:, 512:]
        return gate, upper, (gate * jax.nn.sigmoid(gate) * upper).astype(LOW)

    first, other = lax.optimization_barrier((feed(own), to_core(own)))
    fed = (first, feed(other))
    hidden_whole = (own, other)
    act_low = both(lambda parts: parts[2], fed)

    def feed_out(i):
        return jnp.concatenate([contract(act_low[i], part, 1, 0) for part in down_parts], axis=1)

    dense, _, down = scatter_tokens(feed_out, (), jnp.concatenate(down_parts, axis=1))
    dense_rate = lax.rsqrt(jnp.mean(dense * dense, axis=1, keepdims=True) + EPSILON)
    dense_hat = dense * dense_rate
    output = (hidden + dense_hat * dense_scale).astype(LOW)

    dense_scaled = grad_out * dense_scale
    dense_dot = jnp.mean(dense_scaled * dense_hat, axis=1, keepdims=True)
    dense_back_low = (dense_rate * (dense_scaled - dense_hat * dense_dot)).astype(LOW)
    dense_part = jnp.sum(grad_out * dense_hat, axis=0)

    def back_through(i, rows):
        gate, upper, _ = fed[i]
        act_back = contract(rows, down, 1, 1)
        sigmoid = jax.nn.sigmoid(gate)
        gate_back = act_back * upper * sigmoid * (1.0 + gate * (1.0 - sigmoid))
        up_back = act_back * (gate * sigmoid)
        return jnp.concatenate([gate_back, up_back], axis=1).astype(LOW)

    dense_back, gateup_back_low, (output,), _ = gather_tokens(
        dense_back_low, back_through, ((ungroup, output),)
    )

    def weight_grad(left, right):
        return (contract(left[0], right[0], 0, 0) + contract(left[1], right[1], 0, 0)).astype(LOW)

    grad_down = weight_grad(act_low, dense_back)
    hidden_back, moved, grad_gateup = scatter_tokens(
        lambda i: contract(gateup_back_low[i], gateup_w, 1, 1),
        (
            (give_near, grad_down[:, :HALF]),
            (slice_far, grad_down[:, HALF:]),
        ),
        weight_grad(hidden_whole, gateup_back_low),
    )
    hidden_back = grad_out + hidden_back
    down_parts = moved

    attend_scaled = hidden_back * attend_scale
    attend_dot = jnp.mean(attend_scaled * attend_hat, axis=1, keepdims=True)
    attended_back_low = (attend_rate * (attend_scaled - attend_hat * attend_dot)).astype(LOW)

    attended_back = lax.all_gather(attended_back_low, ("core", "xl", "z"), axis=0, tiled=True)
    mixed_whole = jnp.concatenate(by_core(mixed_low[:512], mixed_low[512:]), axis=0)

    def products(query, query_hat, key, key_hat):
        return jnp.stack([jnp.sum(query * query_hat, axis=1), jnp.sum(key * key_hat, axis=1)])

    def through_norm(rate, scaled, hat, dot):
        return rate * (scaled - hat * dot[:, None])

    def column_sum(first, second):
        return sum(both(lambda a, b: jnp.sum(a * b, axis=0), first, second))

    def attend_whole_back(rows):
        attended_back_low, hidden_back = rows
        attend_part = jnp.sum(hidden_back * attend_hat, axis=0)
        mixed_back = contract(attended_back_low, merge, 1, 1)
        mixed_back_low = to_heads(mixed_back.astype(LOW))
        mixed_back_low = jnp.concatenate(by_core(mixed_back_low[:512], mixed_back_low[512:]))
        query_turned, key_turned, value_back = attend_back(
            core_in, query_low, key_low, value_low, log_total, mixed_back_low
        )
        query_norm_back = both(
            lambda rows, table: rotate_back(rows, *table),
            (query_turned[:512], query_turned[512:]),
            tables,
        )
        value_back = (value_back[:512], value_back[512:])
        key_norm_back = both(
            lambda rows, table: rotate_back(rows, *table),
            (key_turned[:512], key_turned[512:]),
            tables,
        )
        query_scaled = both(lambda rows: rows * query_scale, query_norm_back)
        key_scaled = both(lambda rows: rows * key_scale, key_norm_back)
        parts = jnp.concatenate(
            [
                column_sum(query_norm_back, query_hat)[None],
                column_sum(key_norm_back, key_hat)[None],
                attend_part.reshape(16, 128),
                dense_part.reshape(16, 128),
            ],
            axis=0,
        )
        dots, parts = group_sums(
            *both(products, query_scaled, query_hat, key_scaled, key_hat), parts
        )
        query_back = both(
            through_norm, query_rate, query_scaled, query_hat, (dots[0][0] / D, dots[1][0] / D)
        )
        key_back = both(
            through_norm, key_rate, key_scaled, key_hat, (dots[0][1] / D, dots[1][1] / D)
        )
        back = both(
            lambda *parts: jnp.concatenate(parts, axis=1).astype(LOW),
            query_back,
            key_back,
            value_back,
        )
        return back, parts

    (projected_back_low, parts), moved, _ = beside(
        attend_whole_back,
        (attended_back_low, hidden_back),
        (
            (give_near, grad_gateup[:HALF]),
            (slice_far, grad_gateup[HALF:]),
            (halves_of_sibling, down_parts),
        ),
    )
    down_halves = moved[2]
    projected_back_low, gateup_half = lax.optimization_barrier(
        (projected_back_low, half_of_both(*moved[:2]))
    )
    grad_heads = weight_grad(projected_back_low, whole)
    heads_parts = (give_near(grad_heads[:, :HALF]), slice_far(grad_heads[:, HALF:]))

    first, second = after(grad_heads, projected_back_low)
    arrived = to_core(contract(second, heads, 1, 1).astype(LOW))
    first, arrived = lax.optimization_barrier((contract(first, heads, 1, 1).astype(LOW), arrived))
    mine = add_low(first, arrived)
    attended_back, down_halves, parts = after(mine, (attended_back, down_halves, parts))
    grad_merge = contract(mixed_whole, attended_back, 0, 0).astype(LOW)

    rows = by_slice(parts[:, :2])
    rows = jnp.moveaxis(rows, 1, 0).reshape(4, HALF)
    width = jnp.sum(parts[:, 2:], axis=0).reshape(2, 2, HALF)
    width = jnp.where(high == 0, width, width[:, ::-1]).reshape(4, HALF)
    gains = jnp.concatenate([rows, width, jnp.zeros((24, HALF), WIDE)], axis=0).astype(LOW)
    merge_near = jnp.concatenate([grad_merge[:, :HALF], gains], axis=0)
    merge_far = jnp.concatenate([grad_merge[:, HALF:], gains], axis=0)

    merge_parts = (give_near(merge_near), slice_far(merge_far))
    small_parts = both(lambda *parts: jnp.concatenate(parts, axis=0), heads_parts, merge_parts)
    small_halves = halves_of_sibling(small_parts)
    arrived, gateup_arrived, grad_down = lax.optimization_barrier(
        (exchange(mine), to_sibling(gateup_half), whole_of_half(*down_halves))
    )
    tokens_back = jnp.sum(arrived.reshape(8, SUB, D).astype(WIDE), axis=0)
    grad_tokens = ungroup((hidden_back + tokens_back).astype(LOW))
    small = whole_of_half(*small_halves)
    grad_gateup = whole_of_half(gateup_half, gateup_arrived)
    grad_heads = jnp.swapaxes(small[: 3 * HEAD_DIM], 0, 1)
    grad_merge = small[3 * HEAD_DIM : 4 * HEAD_DIM]
    gains = small[4 * HEAD_DIM : 4 * HEAD_DIM + 8].reshape(4, D)
    return (
        output,
        grad_tokens,
        grad_heads.reshape(HALF, 3, HEAD_DIM),
        grad_merge,
        grad_gateup.reshape(HALF, 2, 512),
        grad_down,
        gains[0],
        gains[1],
        gains[2],
        gains[3],
    )


def solution(mesh):
    fine = Mesh(mesh.devices.reshape(tuple(SIZES[name] for name in NAMES)), NAMES)
    dp, row, col = ("yl", "core"), ("xh", "xl", "z"), "yh"
    in_specs = (
        P(dp + row, col),
        P(col, None, row),
        P(row),
        P(row),
        P(row, col),
        P(col),
        P(col, None, row),
        P(row, col),
        P(col),
        P(dp + row, col),
    )
    out_specs = (
        P(dp + row, col),
        P(dp + row, col),
        P(col, None, row),
        P(row, col),
        P(col, None, row),
        P(row, col),
        P(),
        P(),
        P(),
        P(),
    )
    return jax.shard_map(local, mesh=fine, in_specs=in_specs, out_specs=out_specs, check_vma=False)
```

```python
import itertools

import jax
import jax.numpy as jnp
from jax import lax
from jax.experimental import pallas as pl
from jax.experimental.pallas import tpu as pltpu
from jax.sharding import Mesh
from jax.sharding import PartitionSpec as P

D = 2048
HEAD_DIM = 128
SEQ_LEN = 1024
HALF = 1024
SUB = 64
EPSILON = 1e-06
THETA = 500000.0
NEGATIVE = -1e30

LOW = jnp.bfloat16
WIDE = jnp.float32

NAMES = ("yl", "core", "xh", "xl", "z", "yh")
SIZES = {"yl": 2, "core": 2, "xh": 2, "xl": 2, "z": 4, "yh": 2}


def contract(left, right, left_dim, right_dim):
    return lax.dot_general(
        left, right, (((left_dim,), (right_dim,)), ((), ())), preferred_element_type=WIDE
    )


def pairs_of(axes, target):
    sizes = [SIZES[name] for name in axes]

    def flat(place):
        index = 0
        for value, size in zip(place, sizes):
            index = index * size + value
        return index

    return [
        (flat(place), flat(target(*place)))
        for place in itertools.product(*[range(size) for size in sizes])
    ]


def move(value, axes, target):
    return lax.ppermute(value, axes, pairs_of(axes, target))


def to_core(value):
    return move(value, ("core",), lambda c: (1 - c,))


def to_sibling(value):
    return move(value, ("yl",), lambda a: (1 - a,))


def slice_near(value):
    return move(
        value,
        ("core", "xh", "xl"),
        lambda c, a, b: (c, 1 - a, 1 - b) if c == a else (1 - c, a, b),
    )


def give_near(value):
    return move(
        value,
        ("core", "xh", "xl"),
        lambda c, a, b: (1 - c, a, b) if c == a else (c, 1 - a, 1 - b),
    )


def slice_far(value):
    return move(
        value,
        ("yl", "core", "xh", "xl", "yh"),
        lambda l, c, a, b, h: (1 - l, c, a, b, 1 - h)
        if c == a
        else (1 - l, 1 - c, 1 - a, 1 - b, 1 - h),
    )


def after(value, arrays):
    return lax.optimization_barrier((value, arrays))[1]


def beside(function, value, rides, work=()):
    value, arrays = lax.optimization_barrier((value, tuple(array for _, array in rides)))
    moved = tuple(ride(array) for (ride, _), array in zip(rides, arrays))
    return lax.optimization_barrier((function(value), moved, work))


def exchange(rows):
    return lax.all_to_all(rows, ("xl", "z"), 0, 0, tiled=True)


def gather_tokens(shard, function, rides=(), work=()):
    copies = jnp.broadcast_to(shard[None], (8,) + shard.shape).reshape(8 * SUB, shard.shape[1])
    own, moved, work = beside(exchange, copies, rides, work)
    first, other = lax.optimization_barrier((function(0, own), to_core(own)))
    return (own, other), (first, function(1, other)), moved, work


def scatter_tokens(function, rides=(), work=()):
    arrived = to_core(function(1).astype(LOW))
    own, arrived = lax.optimization_barrier((function(0).astype(LOW), arrived))
    arrived, moved, work = beside(exchange, add_low(own, arrived), rides, work)
    total = jnp.sum(arrived.reshape(8, SUB, arrived.shape[1]).astype(WIDE), axis=0)
    return total, moved, work


def by_core(first, second):
    own_first = lax.axis_index("core") == 0
    return jnp.where(own_first, first, second), jnp.where(own_first, second, first)


def group_copies(rows):
    copies = jnp.broadcast_to(rows[None], (16,) + rows.shape).reshape(-1, 128)
    arrived = lax.all_to_all(copies, ("core", "xl", "z"), 0, 0, tiled=True)
    return arrived.reshape((16,) + rows.shape)


def group_sums(own, other, more=None):
    whole = jnp.concatenate(by_core(own, other), axis=0).reshape(16, 128)
    if more is not None:
        whole = jnp.concatenate([whole, more], axis=0)
    arrived = group_copies(whole)
    total = jnp.sum(arrived[:, :16], axis=0).reshape(2, 2, 512)
    return by_core(total[0], total[1]), arrived[:, 16:]


def by_slice(blocks):
    view = blocks.reshape((2, 2, 4) + blocks.shape[1:])
    straight = jnp.arange(2) == lax.axis_index("xh")
    straight = straight.reshape((2,) + (1,) * (view.ndim - 2))
    first = jnp.where(straight, view[:, 0], view[:, 1])
    second = jnp.where(straight, view[:, 1], view[:, 0])
    return jnp.stack([first, second], axis=1).reshape(blocks.shape)


def to_owners(own, other):
    blocks = jnp.concatenate(by_core(own, other), axis=0)
    arrived = lax.all_to_all(blocks, ("core", "xl", "z"), 0, 0, tiled=True)
    return jnp.swapaxes(arrived.reshape(16, SUB, HEAD_DIM), 0, 1).reshape(SUB, D)


def to_heads(rows):
    blocks = jnp.swapaxes(rows.reshape(SUB, 16, HEAD_DIM), 0, 1).reshape(16 * SUB, HEAD_DIM)
    return lax.all_to_all(blocks, ("core", "xl", "z"), 0, 0, tiled=True)


def both(function, *pairs):
    return tuple(function(*items) for items in zip(*pairs))


def add_low(first, *others):
    total = first.astype(WIDE)
    for other in others:
        total = total + other.astype(WIDE)
    return total.astype(LOW)


def regroup(block):
    core = lax.axis_index("core")
    high = lax.axis_index("yh")
    lower, upper = block[:SUB], block[SUB:]
    parts = []
    for j in (0, 1):
        piece = jnp.where((high ^ j) == 0, lower, upper)
        parts.append(move(piece, ("core", "yh"), lambda c, h: (h ^ j, c)))
    same = core == high
    return jnp.concatenate(
        [jnp.where(same, parts[0], parts[1]), jnp.where(same, parts[1], parts[0])], axis=1
    )


def ungroup(block):
    core = lax.axis_index("core")
    high = lax.axis_index("yh")
    near, far = block[:, :HALF], block[:, HALF:]
    parts = []
    for j in (0, 1):
        piece = jnp.where((core ^ j) == high, near, far)
        parts.append(move(piece, ("core", "yh"), lambda c, h: (h, c ^ j)))
    first = high == 0
    return jnp.concatenate(
        [jnp.where(first, parts[0], parts[1]), jnp.where(first, parts[1], parts[0])], axis=0
    )


def half_of_both(arrived_near, arrived_far):
    part = arrived_near.astype(WIDE) + arrived_far.astype(WIDE)
    rows = part.shape[0] // 2
    core = lax.axis_index("core")
    lower, upper = part[:rows], part[rows:]
    keep = jnp.where(core == 0, lower, upper)
    give = jnp.where(core == 0, upper, lower).astype(LOW)
    return (keep + to_core(give).astype(WIDE)).astype(LOW)


def halves_of_sibling(parts):
    half = half_of_both(*parts)
    return half, to_sibling(half)


def whole_of_half(half, arrived):
    core = lax.axis_index("core")
    half = add_low(half, arrived)
    other = to_core(half)
    return jnp.concatenate(
        [jnp.where(core == 0, half, other), jnp.where(core == 0, other, half)], axis=0
    )


def rope_tables(place):
    pairs = HEAD_DIM // 2
    freq = THETA ** (-(jnp.arange(pairs, dtype=WIDE) * (2.0 / HEAD_DIM)))
    angle = place.astype(WIDE)[:, None] * freq[None, :]
    cosine = jnp.concatenate([jnp.cos(angle), jnp.cos(angle)], axis=1)
    sine = jnp.concatenate([jnp.sin(angle), jnp.sin(angle)], axis=1)
    return (cosine, sine)


def rotate(values, cosine, sine):
    pairs = HEAD_DIM // 2
    turned = jnp.concatenate([-values[:, pairs:], values[:, :pairs]], axis=1)
    return values * cosine + turned * sine


def rotate_back(grad, cosine, sine):
    pairs = HEAD_DIM // 2
    scaled = grad * sine
    turned = jnp.concatenate([scaled[:, pairs:], -scaled[:, :pairs]], axis=1)
    return grad * cosine + turned


ROWS = 256
SCALE = HEAD_DIM ** (-0.5)


def places_of(index, core):
    block, row = (index % 512) // SUB, index % SUB
    return block * 128 + jnp.where(index < 512, core, 1 - core) * SUB + row


def block_scores(core_ref, query, key):
    first = pl.program_id(0) * ROWS
    query_index = first + lax.broadcasted_iota(jnp.int32, (ROWS, 1), 0)
    key_index = lax.broadcasted_iota(jnp.int32, (1, SEQ_LEN), 1)
    core = core_ref[0]
    allowed = places_of(key_index, core) <= places_of(query_index, core)
    return jnp.where(allowed, contract(query, key, 1, 1) * SCALE, NEGATIVE)


def attend_kernel(core_ref, query_ref, key_ref, value_ref, mixed_ref, total_ref):
    scores = block_scores(core_ref, query_ref[...], key_ref[...])
    top = jnp.max(scores, axis=1, keepdims=True)
    shifted = jnp.exp(scores - top)
    total = jnp.sum(shifted, axis=1, keepdims=True)
    probs_low = (shifted * (1.0 / total)).astype(LOW)
    mixed_ref[...] = contract(probs_low, value_ref[...], 1, 0).astype(LOW)
    total_ref[...] = jnp.broadcast_to(top + jnp.log(total), total_ref.shape)


def attend_back_kernel(
    core_ref,
    query_ref,
    key_ref,
    value_ref,
    total_ref,
    mixed_back_ref,
    query_out,
    key_out,
    value_out,
):
    query, key, mixed_back = query_ref[...], key_ref[...], mixed_back_ref[...]
    probs = jnp.exp(block_scores(core_ref, query, key) - total_ref[...][:, :1])
    probs_back = contract(mixed_back, value_ref[...], 1, 1)
    row_dot = jnp.sum(probs_back * probs, axis=1, keepdims=True)
    scores_back = (probs * (probs_back - row_dot)).astype(LOW)
    query_out[...] = contract(scores_back, key, 1, 0) * SCALE
    key_part = contract(scores_back, query, 0, 0) * SCALE
    value_part = contract(probs.astype(LOW), mixed_back, 0, 0)

    @pl.when(pl.program_id(0) == 0)
    def _():
        key_out[...] = key_part
        value_out[...] = value_part

    @pl.when(pl.program_id(0) > 0)
    def _():
        key_out[...] += key_part
        value_out[...] += value_part


def row_spec():
    return pl.BlockSpec((ROWS, HEAD_DIM), lambda i: (i, 0))


def whole_spec():
    return pl.BlockSpec((SEQ_LEN, HEAD_DIM), lambda i: (0, 0))


def core_spec():
    return pl.BlockSpec(memory_space=pltpu.SMEM)


def head_call(kernel, in_specs, out_specs, out_types):
    return pl.pallas_call(
        kernel,
        grid=(SEQ_LEN // ROWS,),
        in_specs=in_specs,
        out_specs=out_specs,
        out_shape=[jax.ShapeDtypeStruct((SEQ_LEN, HEAD_DIM), kind) for kind in out_types],
        compiler_params=pltpu.CompilerParams(vmem_limit_bytes=32 * 1024 * 1024),
        cost_estimate=pl.CostEstimate(flops=0, bytes_accessed=0, transcendentals=0),
    )


def attend(core, query, key, value):
    return head_call(
        attend_kernel,
        [core_spec(), row_spec(), whole_spec(), whole_spec()],
        [row_spec(), row_spec()],
        [LOW, WIDE],
    )(core, query, key, value)


def attend_back(core, query, key, value, total, mixed_back):
    return head_call(
        attend_back_kernel,
        [core_spec(), row_spec(), whole_spec(), whole_spec(), row_spec(), row_spec()],
        [row_spec(), whole_spec(), whole_spec()],
        [WIDE, WIDE, WIDE],
    )(core, query, key, value, total, mixed_back)


def spread_kernel(rows_ref, heads_ref):
    for i in range(3):
        part = rows_ref[i * HEAD_DIM : (i + 1) * HEAD_DIM, :]
        heads_ref[:, i, :] = jnp.transpose(part.astype(WIDE))


def spread_heads(rows):
    return pl.pallas_call(
        spread_kernel,
        grid=(2,),
        in_specs=[pl.BlockSpec((3 * HEAD_DIM, 512), lambda i: (0, i))],
        out_specs=pl.BlockSpec((512, 3, HEAD_DIM), lambda i: (i, 0, 0)),
        out_shape=jax.ShapeDtypeStruct((HALF, 3, HEAD_DIM), WIDE),
        compiler_params=pltpu.CompilerParams(vmem_limit_bytes=32 * 1024 * 1024),
    )(rows)


def spread_gateup_kernel(rows_ref, gateup_ref):
    for i in range(2):
        gateup_ref[:, i, :] = rows_ref[:, i * 512 : (i + 1) * 512].astype(WIDE)


def spread_gateup(rows):
    return pl.pallas_call(
        spread_gateup_kernel,
        grid=(4,),
        in_specs=[pl.BlockSpec((256, HALF), lambda i: (i, 0))],
        out_specs=pl.BlockSpec((256, 2, 512), lambda i: (i, 0, 0)),
        out_shape=jax.ShapeDtypeStruct((HALF, 2, 512), WIDE),
        compiler_params=pltpu.CompilerParams(vmem_limit_bytes=32 * 1024 * 1024),
    )(rows)


def local(
    tokens,
    w_heads,
    query_scale,
    key_scale,
    w_merge,
    attend_scale,
    w_gateup,
    w_down,
    dense_scale,
    cotangent,
):
    core = lax.axis_index("core")
    xh = lax.axis_index("xh")
    xl = lax.axis_index("xl")
    z = lax.axis_index("z")
    high = lax.axis_index("yh")

    shard = regroup(tokens)
    heads_in = w_heads.reshape(HALF, 3 * HEAD_DIM)
    gateup_in = w_gateup.reshape(HALF, 2 * 512)

    index = jnp.arange(512, dtype=jnp.int32)
    place = index // SUB * 128 + index % SUB
    places = (place + core * SUB, place + (1 - core) * SUB)
    tables = both(rope_tables, places)
    core_in = core.astype(jnp.int32)[None]

    copies = jnp.broadcast_to(shard[None], (8,) + shard.shape).reshape(8 * SUB, D)
    merge_in = after(copies, w_merge)
    merge_parts = (slice_near(merge_in), slice_far(merge_in))
    own, moved, (tables, gateup_in, merge) = beside(
        exchange,
        copies,
        (
            (slice_near, heads_in),
            (slice_far, heads_in),
        ),
        (tables, gateup_in, jnp.concatenate(merge_parts, axis=1)),
    )
    head_scales, width_scales = after(
        own, (jnp.stack([query_scale, key_scale]), jnp.stack([attend_scale, dense_scale]))
    )
    query_scale, key_scale = slice_near(head_scales)
    attend_scale, dense_scale = jnp.concatenate(
        [width_scales, move(width_scales, ("yl", "yh"), lambda l, h: (1 - l, 1 - h))], axis=1
    )
    heads = jnp.concatenate(moved, axis=0)
    merge = lax.all_gather(merge, ("core", "xl", "z"), axis=0, tiled=True)

    def squares(query, key):
        return jnp.stack([jnp.sum(query * query, axis=1), jnp.sum(key * key, axis=1)])

    def attend_whole(own):
        first, other = lax.optimization_barrier((contract(own, heads, 1, 0), to_core(own)))
        projected = (first, contract(other, heads, 1, 0))
        query_raw = both(lambda rows: rows[:, :HEAD_DIM], projected)
        key_raw = both(lambda rows: rows[:, HEAD_DIM : 2 * HEAD_DIM], projected)
        value_low = jnp.concatenate(
            both(lambda rows: rows[:, 2 * HEAD_DIM :].astype(LOW), projected), axis=0
        )
        powers, _ = group_sums(*both(squares, query_raw, key_raw))
        rates = both(lambda rows: lax.rsqrt(rows / D + EPSILON), powers)
        query_rate = both(lambda rows: rows[0][:, None], rates)
        key_rate = both(lambda rows: rows[1][:, None], rates)
        query_hat = both(lambda raw, rate: raw * rate, query_raw, query_rate)
        key_hat = both(lambda raw, rate: raw * rate, key_raw, key_rate)
        query_low = jnp.concatenate(
            both(
                lambda hat, table: rotate(hat * query_scale, *table).astype(LOW), query_hat, tables
            ),
            axis=0,
        )
        key_low = jnp.concatenate(
            both(lambda hat, table: rotate(hat * key_scale, *table).astype(LOW), key_hat, tables),
            axis=0,
        )

        mixed_low, log_total = attend(core_in, query_low, key_low, value_low)
        attended = contract(to_owners(mixed_low[:512], mixed_low[512:]), merge, 1, 0)
        return (
            (own, other),
            (query_rate, key_rate, query_hat, key_hat),
            (query_low, key_low, value_low),
            mixed_low,
            log_total,
            attended,
        )

    (whole, norms, lows, mixed_low, log_total, attended), gateup_parts, _ = beside(
        attend_whole, own, ((slice_near, gateup_in), (slice_far, gateup_in))
    )
    query_rate, key_rate, query_hat, key_hat = norms
    query_low, key_low, value_low = lows
    attend_rate = lax.rsqrt(jnp.mean(attended * attended, axis=1, keepdims=True) + EPSILON)
    attend_hat = attended * attend_rate
    hidden = shard.astype(WIDE) + attend_hat * attend_scale

    copies = jnp.broadcast_to(hidden.astype(LOW)[None], (8, SUB, D)).reshape(8 * SUB, D)
    own, down_parts, gateup_w = beside(
        exchange,
        copies,
        ((slice_near, w_down), (slice_far, w_down)),
        jnp.concatenate(gateup_parts, axis=0),
    )

    def feed(rows):
        gateup = contract(rows, gateup_w, 1, 0)
        gate, upper = gateup[:, :512], gateup[:, 512:]
        return gate, upper, (gate * jax.nn.sigmoid(gate) * upper).astype(LOW)

    first, other = lax.optimization_barrier((feed(own), to_core(own)))
    fed = (first, feed(other))
    hidden_whole = (own, other)
    act_low = both(lambda parts: parts[2], fed)

    def feed_out(i):
        return jnp.concatenate([contract(act_low[i], part, 1, 0) for part in down_parts], axis=1)

    dense, (grad_out,), down = scatter_tokens(
        feed_out, ((regroup, cotangent),), jnp.concatenate(down_parts, axis=1)
    )
    grad_out = grad_out.astype(WIDE)
    dense_rate = lax.rsqrt(jnp.mean(dense * dense, axis=1, keepdims=True) + EPSILON)
    dense_hat = dense * dense_rate
    output = (hidden + dense_hat * dense_scale).astype(LOW)

    dense_scaled = grad_out * dense_scale
    dense_dot = jnp.mean(dense_scaled * dense_hat, axis=1, keepdims=True)
    dense_back_low = (dense_rate * (dense_scaled - dense_hat * dense_dot)).astype(LOW)
    dense_part = jnp.sum(grad_out * dense_hat, axis=0)

    def back_through(i, rows):
        gate, upper, _ = fed[i]
        act_back = contract(rows, down, 1, 1)
        sigmoid = jax.nn.sigmoid(gate)
        gate_back = act_back * upper * sigmoid * (1.0 + gate * (1.0 - sigmoid))
        up_back = act_back * (gate * sigmoid)
        return jnp.concatenate([gate_back, up_back], axis=1).astype(LOW)

    dense_back, gateup_back_low, (output,), _ = gather_tokens(
        dense_back_low, back_through, ((ungroup, output),)
    )

    def weight_grad(left, right):
        return (contract(left[0], right[0], 0, 0) + contract(left[1], right[1], 0, 0)).astype(LOW)

    grad_down = weight_grad(act_low, dense_back)
    hidden_back, moved, grad_gateup = scatter_tokens(
        lambda i: contract(gateup_back_low[i], gateup_w, 1, 1),
        (
            (give_near, grad_down[:, :HALF]),
            (slice_far, grad_down[:, HALF:]),
        ),
        weight_grad(hidden_whole, gateup_back_low),
    )
    hidden_back = grad_out + hidden_back
    down_parts = moved

    attend_scaled = hidden_back * attend_scale
    attend_dot = jnp.mean(attend_scaled * attend_hat, axis=1, keepdims=True)
    attended_back_low = (attend_rate * (attend_scaled - attend_hat * attend_dot)).astype(LOW)

    attended_back = lax.all_gather(attended_back_low, ("core", "xl", "z"), axis=0, tiled=True)
    mixed_whole = jnp.concatenate(by_core(mixed_low[:512], mixed_low[512:]), axis=0)

    def products(query, query_hat, key, key_hat):
        return jnp.stack([jnp.sum(query * query_hat, axis=1), jnp.sum(key * key_hat, axis=1)])

    def through_norm(rate, scaled, hat, dot):
        return rate * (scaled - hat * dot[:, None])

    def column_sum(first, second):
        return sum(both(lambda a, b: jnp.sum(a * b, axis=0), first, second))

    def attend_whole_back(rows, gateup_parts):
        attended_back_low, hidden_back = rows
        attend_part = jnp.sum(hidden_back * attend_hat, axis=0)
        mixed_back = contract(attended_back_low, merge, 1, 1)
        mixed_back_low = to_heads(mixed_back.astype(LOW))
        mixed_back_low = jnp.concatenate(by_core(mixed_back_low[:512], mixed_back_low[512:]))
        (query_turned, key_turned, value_back), gateup_parts = lax.optimization_barrier(
            (
                attend_back(core_in, query_low, key_low, value_low, log_total, mixed_back_low),
                gateup_parts,
            )
        )
        query_norm_back = both(
            lambda rows, table: rotate_back(rows, *table),
            (query_turned[:512], query_turned[512:]),
            tables,
        )
        value_back = (value_back[:512], value_back[512:])
        key_norm_back = both(
            lambda rows, table: rotate_back(rows, *table),
            (key_turned[:512], key_turned[512:]),
            tables,
        )
        query_scaled = both(lambda rows: rows * query_scale, query_norm_back)
        key_scaled = both(lambda rows: rows * key_scale, key_norm_back)
        parts = jnp.concatenate(
            [
                column_sum(query_norm_back, query_hat)[None],
                column_sum(key_norm_back, key_hat)[None],
                attend_part.reshape(16, 128),
                dense_part.reshape(16, 128),
            ],
            axis=0,
        )
        dots, parts = group_sums(
            *both(products, query_scaled, query_hat, key_scaled, key_hat), parts
        )
        query_back = both(
            through_norm, query_rate, query_scaled, query_hat, (dots[0][0] / D, dots[1][0] / D)
        )
        key_back = both(
            through_norm, key_rate, key_scaled, key_hat, (dots[0][1] / D, dots[1][1] / D)
        )
        back = both(
            lambda *parts: jnp.concatenate(parts, axis=1).astype(LOW),
            query_back,
            key_back,
            value_back,
        )
        return back, parts, half_of_both(*gateup_parts)

    rows_in, ride_in = lax.optimization_barrier(
        (
            (attended_back_low, hidden_back),
            (grad_gateup[:HALF], grad_gateup[HALF:], down_parts),
        )
    )
    gateup_parts = (give_near(ride_in[0]), slice_far(ride_in[1]))
    down_halves = halves_of_sibling(ride_in[2])
    projected_back_low, parts, gateup_half, down_halves = lax.optimization_barrier(
        (*attend_whole_back(rows_in, gateup_parts), down_halves)
    )
    grad_heads = weight_grad(projected_back_low, whole)
    heads_parts = (give_near(grad_heads[:, :HALF]), slice_far(grad_heads[:, HALF:]))

    first, second = after(grad_heads, projected_back_low)
    arrived = to_core(contract(second, heads, 1, 1).astype(LOW))
    first, arrived = lax.optimization_barrier((contract(first, heads, 1, 1).astype(LOW), arrived))
    mine = add_low(first, arrived)
    attended_back, down_halves, parts = after(mine, (attended_back, down_halves, parts))
    grad_merge = contract(mixed_whole, attended_back, 0, 0).astype(LOW)

    rows = by_slice(parts[:, :2])
    rows = jnp.moveaxis(rows, 1, 0).reshape(4, HALF)
    width = jnp.sum(parts[:, 2:], axis=0).reshape(2, 2, HALF)
    width = jnp.where(high == 0, width, width[:, ::-1]).reshape(4, HALF)
    gains = jnp.concatenate([rows, width, jnp.zeros((24, HALF), WIDE)], axis=0).astype(LOW)
    merge_near = jnp.concatenate([grad_merge[:, :HALF], gains], axis=0)
    merge_far = jnp.concatenate([grad_merge[:, HALF:], gains], axis=0)

    merge_parts = (give_near(merge_near), slice_far(merge_far))
    small_parts = both(lambda *parts: jnp.concatenate(parts, axis=0), heads_parts, merge_parts)
    small_parts, gateup_arrived = lax.optimization_barrier(
        (small_parts, to_sibling(gateup_half))
    )
    arrived, grad_down, small_half = lax.optimization_barrier(
        (
            exchange(mine),
            whole_of_half(*down_halves).astype(WIDE),
            half_of_both(*small_parts),
        )
    )
    tokens_back = jnp.sum(arrived.reshape(8, SUB, D).astype(WIDE), axis=0)
    small_arrived, grad_gateup, grad_tokens = lax.optimization_barrier(
        (
            to_sibling(small_half),
            spread_gateup(whole_of_half(gateup_half, gateup_arrived)),
            ungroup((hidden_back + tokens_back).astype(LOW)),
        )
    )
    small = whole_of_half(small_half, small_arrived)
    grad_heads = spread_heads(small)
    grad_merge = small[3 * HEAD_DIM : 4 * HEAD_DIM].astype(WIDE)
    gains = small[4 * HEAD_DIM : 4 * HEAD_DIM + 8].astype(WIDE).reshape(4, D)
    return (
        output,
        grad_tokens,
        grad_heads,
        grad_merge,
        grad_gateup,
        grad_down,
        gains[0],
        gains[1],
        gains[2],
        gains[3],
    )


def solution(mesh):
    fine = Mesh(mesh.devices.reshape(tuple(SIZES[name] for name in NAMES)), NAMES)
    dp, row, col = ("yl", "core"), ("xh", "xl", "z"), "yh"
    in_specs = (
        P(dp + row, col),
        P(col, None, row),
        P(row),
        P(row),
        P(row, col),
        P(col),
        P(col, None, row),
        P(row, col),
        P(col),
        P(dp + row, col),
    )
    out_specs = (
        P(dp + row, col),
        P(dp + row, col),
        P(col, None, row),
        P(row, col),
        P(col, None, row),
        P(row, col),
        P(),
        P(),
        P(),
        P(),
    )
    return jax.shard_map(local, mesh=fine, in_specs=in_specs, out_specs=out_specs, check_vma=False)
```

```python
import itertools

import jax
import jax.numpy as jnp
from jax import lax
from jax.experimental import pallas as pl
from jax.experimental.pallas import tpu as pltpu
from jax.sharding import Mesh
from jax.sharding import PartitionSpec as P

D = 2048
HEAD_DIM = 128
SEQ_LEN = 1024
HALF = 1024
SUB = 64
EPSILON = 1e-06
THETA = 500000.0
NEGATIVE = -1e30

LOW = jnp.bfloat16
WIDE = jnp.float32

NAMES = ("yl", "core", "xh", "xl", "z", "yh")
SIZES = {"yl": 2, "core": 2, "xh": 2, "xl": 2, "z": 4, "yh": 2}


def contract(left, right, left_dim, right_dim):
    return lax.dot_general(
        left, right, (((left_dim,), (right_dim,)), ((), ())), preferred_element_type=WIDE
    )


def pairs_of(axes, target):
    sizes = [SIZES[name] for name in axes]

    def flat(place):
        index = 0
        for value, size in zip(place, sizes):
            index = index * size + value
        return index

    return [
        (flat(place), flat(target(*place)))
        for place in itertools.product(*[range(size) for size in sizes])
    ]


def move(value, axes, target):
    return lax.ppermute(value, axes, pairs_of(axes, target))


def to_core(value):
    return move(value, ("core",), lambda c: (1 - c,))


def to_sibling(value):
    return move(value, ("yl",), lambda a: (1 - a,))


def slice_near(value):
    return move(
        value,
        ("core", "xh", "xl"),
        lambda c, a, b: (c, 1 - a, 1 - b) if c == a else (1 - c, a, b),
    )


def give_near(value):
    return move(
        value,
        ("core", "xh", "xl"),
        lambda c, a, b: (1 - c, a, b) if c == a else (c, 1 - a, 1 - b),
    )


def slice_far(value):
    return move(
        value,
        ("yl", "core", "xh", "xl", "yh"),
        lambda l, c, a, b, h: (1 - l, c, a, b, 1 - h)
        if c == a
        else (1 - l, 1 - c, 1 - a, 1 - b, 1 - h),
    )


def after(value, arrays):
    return lax.optimization_barrier((value, arrays))[1]


def beside(function, value, rides, work=()):
    value, arrays = lax.optimization_barrier((value, tuple(array for _, array in rides)))
    moved = tuple(ride(array) for (ride, _), array in zip(rides, arrays))
    return lax.optimization_barrier((function(value), moved, work))


def exchange(rows):
    return lax.all_to_all(rows, ("xl", "z"), 0, 0, tiled=True)


def scatter_parts(function, rides=()):
    arrived = to_core(function(1))
    own, arrived = lax.optimization_barrier((function(0), arrived))
    arrived, moved, _ = beside(exchange, add_low(own, arrived), rides)
    return arrived, moved


def by_core(first, second):
    own_first = lax.axis_index("core") == 0
    return jnp.where(own_first, first, second), jnp.where(own_first, second, first)


def group_copies(rows):
    copies = jnp.broadcast_to(rows[None], (16,) + rows.shape).reshape(-1, 128)
    arrived = lax.all_to_all(copies, ("core", "xl", "z"), 0, 0, tiled=True)
    return arrived.reshape((16,) + rows.shape)


def group_sums(own, other, more=None):
    whole = jnp.concatenate(by_core(own, other), axis=0).reshape(16, 128)
    if more is not None:
        whole = jnp.concatenate([whole, more], axis=0)
    arrived = group_copies(whole)
    total = jnp.sum(arrived[:, :16], axis=0).reshape(2, 2, 512)
    return by_core(total[0], total[1]), arrived[:, 16:]


def by_slice(blocks):
    view = blocks.reshape((2, 2, 4) + blocks.shape[1:])
    straight = jnp.arange(2) == lax.axis_index("xh")
    straight = straight.reshape((2,) + (1,) * (view.ndim - 2))
    first = jnp.where(straight, view[:, 0], view[:, 1])
    second = jnp.where(straight, view[:, 1], view[:, 0])
    return jnp.stack([first, second], axis=1).reshape(blocks.shape)


def to_owners(own, other):
    blocks = jnp.concatenate(by_core(own, other), axis=0)
    arrived = lax.all_to_all(blocks, ("core", "xl", "z"), 0, 0, tiled=True)
    return jnp.swapaxes(arrived.reshape(16, SUB, HEAD_DIM), 0, 1).reshape(SUB, D)


def to_heads(rows):
    blocks = jnp.swapaxes(rows.reshape(SUB, 16, HEAD_DIM), 0, 1).reshape(16 * SUB, HEAD_DIM)
    return lax.all_to_all(blocks, ("core", "xl", "z"), 0, 0, tiled=True)


def both(function, *pairs):
    return tuple(function(*items) for items in zip(*pairs))


def halves(pair):
    return tuple(rows[:, :HALF] for rows in pair), tuple(rows[:, HALF:] for rows in pair)


def add_low(first, *others):
    total = first.astype(WIDE)
    for other in others:
        total = total + other.astype(WIDE)
    return total.astype(LOW)


def regroup(block):
    core = lax.axis_index("core")
    high = lax.axis_index("yh")
    lower, upper = block[:SUB], block[SUB:]
    parts = []
    for j in (0, 1):
        piece = jnp.where((high ^ j) == 0, lower, upper)
        parts.append(move(piece, ("core", "yh"), lambda c, h: (h ^ j, c)))
    same = core == high
    return jnp.concatenate(
        [jnp.where(same, parts[0], parts[1]), jnp.where(same, parts[1], parts[0])], axis=1
    )


def ungroup(block):
    core = lax.axis_index("core")
    high = lax.axis_index("yh")
    near, far = block[:, :HALF], block[:, HALF:]
    parts = []
    for j in (0, 1):
        piece = jnp.where((core ^ j) == high, near, far)
        parts.append(move(piece, ("core", "yh"), lambda c, h: (h, c ^ j)))
    first = high == 0
    return jnp.concatenate(
        [jnp.where(first, parts[0], parts[1]), jnp.where(first, parts[1], parts[0])], axis=0
    )


def half_of_both(arrived_near, arrived_far):
    part = arrived_near.astype(WIDE) + arrived_far.astype(WIDE)
    rows = part.shape[0] // 2
    core = lax.axis_index("core")
    lower, upper = part[:rows], part[rows:]
    keep = jnp.where(core == 0, lower, upper)
    give = jnp.where(core == 0, upper, lower).astype(LOW)
    return (keep + to_core(give).astype(WIDE)).astype(LOW)


def halves_of_sibling(parts):
    half = half_of_both(*parts)
    return half, to_sibling(half)


def whole_of_half(half, arrived):
    core = lax.axis_index("core")
    half = add_low(half, arrived)
    other = to_core(half)
    return jnp.concatenate(
        [jnp.where(core == 0, half, other), jnp.where(core == 0, other, half)], axis=0
    )


def rope_tables(place):
    pairs = HEAD_DIM // 2
    freq = THETA ** (-(jnp.arange(pairs, dtype=WIDE) * (2.0 / HEAD_DIM)))
    angle = place.astype(WIDE)[:, None] * freq[None, :]
    cosine = jnp.concatenate([jnp.cos(angle), jnp.cos(angle)], axis=1)
    sine = jnp.concatenate([jnp.sin(angle), jnp.sin(angle)], axis=1)
    return (cosine, sine)


def rotate(values, cosine, sine):
    pairs = HEAD_DIM // 2
    turned = jnp.concatenate([-values[:, pairs:], values[:, :pairs]], axis=1)
    return values * cosine + turned * sine


def rotate_back(grad, cosine, sine):
    pairs = HEAD_DIM // 2
    scaled = grad * sine
    turned = jnp.concatenate([scaled[:, pairs:], -scaled[:, :pairs]], axis=1)
    return grad * cosine + turned


ROWS = 256
SCALE = HEAD_DIM ** (-0.5)


def places_of(index, core):
    block, row = (index % 512) // SUB, index % SUB
    return block * 128 + jnp.where(index < 512, core, 1 - core) * SUB + row


def block_scores(core_ref, query, key):
    first = pl.program_id(0) * ROWS
    query_index = first + lax.broadcasted_iota(jnp.int32, (ROWS, 1), 0)
    key_index = lax.broadcasted_iota(jnp.int32, (1, SEQ_LEN), 1)
    core = core_ref[0]
    allowed = places_of(key_index, core) <= places_of(query_index, core)
    return jnp.where(allowed, contract(query, key, 1, 1) * SCALE, NEGATIVE)


def attend_kernel(core_ref, query_ref, key_ref, value_ref, mixed_ref, total_ref):
    scores = block_scores(core_ref, query_ref[...], key_ref[...])
    top = jnp.max(scores, axis=1, keepdims=True)
    shifted = jnp.exp(scores - top)
    total = jnp.sum(shifted, axis=1, keepdims=True)
    probs_low = (shifted * (1.0 / total)).astype(LOW)
    mixed_ref[...] = contract(probs_low, value_ref[...], 1, 0).astype(LOW)
    total_ref[...] = jnp.broadcast_to(top + jnp.log(total), total_ref.shape)


def attend_back_kernel(
    core_ref,
    query_ref,
    key_ref,
    value_ref,
    total_ref,
    mixed_back_ref,
    query_out,
    key_out,
    value_out,
):
    query, key, mixed_back = query_ref[...], key_ref[...], mixed_back_ref[...]
    probs = jnp.exp(block_scores(core_ref, query, key) - total_ref[...][:, :1])
    probs_back = contract(mixed_back, value_ref[...], 1, 1)
    row_dot = jnp.sum(probs_back * probs, axis=1, keepdims=True)
    scores_back = (probs * (probs_back - row_dot)).astype(LOW)
    query_out[...] = contract(scores_back, key, 1, 0) * SCALE
    key_part = contract(scores_back, query, 0, 0) * SCALE
    value_part = contract(probs.astype(LOW), mixed_back, 0, 0)

    @pl.when(pl.program_id(0) == 0)
    def _():
        key_out[...] = key_part
        value_out[...] = value_part

    @pl.when(pl.program_id(0) > 0)
    def _():
        key_out[...] += key_part
        value_out[...] += value_part


def row_spec():
    return pl.BlockSpec((ROWS, HEAD_DIM), lambda i: (i, 0))


def whole_spec():
    return pl.BlockSpec((SEQ_LEN, HEAD_DIM), lambda i: (0, 0))


def core_spec():
    return pl.BlockSpec(memory_space=pltpu.SMEM)


def head_call(kernel, in_specs, out_specs, out_types):
    return pl.pallas_call(
        kernel,
        grid=(SEQ_LEN // ROWS,),
        in_specs=in_specs,
        out_specs=out_specs,
        out_shape=[jax.ShapeDtypeStruct((SEQ_LEN, HEAD_DIM), kind) for kind in out_types],
        compiler_params=pltpu.CompilerParams(vmem_limit_bytes=32 * 1024 * 1024),
        cost_estimate=pl.CostEstimate(flops=0, bytes_accessed=0, transcendentals=0),
    )


def attend(core, query, key, value):
    return head_call(
        attend_kernel,
        [core_spec(), row_spec(), whole_spec(), whole_spec()],
        [row_spec(), row_spec()],
        [LOW, WIDE],
    )(core, query, key, value)


def attend_back(core, query, key, value, total, mixed_back):
    return head_call(
        attend_back_kernel,
        [core_spec(), row_spec(), whole_spec(), whole_spec(), row_spec(), row_spec()],
        [row_spec(), whole_spec(), whole_spec()],
        [WIDE, WIDE, WIDE],
    )(core, query, key, value, total, mixed_back)


def spread_kernel(rows_ref, heads_ref):
    for i in range(3):
        part = rows_ref[i * HEAD_DIM : (i + 1) * HEAD_DIM, :]
        heads_ref[:, i, :] = jnp.transpose(part.astype(WIDE))


def spread_heads(rows):
    return pl.pallas_call(
        spread_kernel,
        grid=(2,),
        in_specs=[pl.BlockSpec((3 * HEAD_DIM, 512), lambda i: (0, i))],
        out_specs=pl.BlockSpec((512, 3, HEAD_DIM), lambda i: (i, 0, 0)),
        out_shape=jax.ShapeDtypeStruct((HALF, 3, HEAD_DIM), WIDE),
        compiler_params=pltpu.CompilerParams(vmem_limit_bytes=32 * 1024 * 1024),
    )(rows)


def spread_gateup_kernel(rows_ref, gateup_ref):
    for i in range(2):
        gateup_ref[:, i, :] = rows_ref[:, i * 512 : (i + 1) * 512].astype(WIDE)


def spread_gateup(rows):
    return pl.pallas_call(
        spread_gateup_kernel,
        grid=(4,),
        in_specs=[pl.BlockSpec((256, HALF), lambda i: (i, 0))],
        out_specs=pl.BlockSpec((256, 2, 512), lambda i: (i, 0, 0)),
        out_shape=jax.ShapeDtypeStruct((HALF, 2, 512), WIDE),
        compiler_params=pltpu.CompilerParams(vmem_limit_bytes=32 * 1024 * 1024),
    )(rows)


LIMIT = pltpu.CompilerParams(vmem_limit_bytes=40 * 1024 * 1024)


def estimate(flops, moved):
    return pl.CostEstimate(flops=flops, bytes_accessed=moved, transcendentals=0)


def feed_kernel(rows_ref, gate_w_ref, upper_w_ref, gate_ref, upper_ref, act_ref):
    rows = rows_ref[...]
    gate = contract(rows, gate_w_ref[...], 1, 0)
    upper = contract(rows, upper_w_ref[...], 1, 0)
    gate_ref[...] = gate
    upper_ref[...] = upper
    act_ref[...] = (gate * jax.nn.sigmoid(gate) * upper).astype(LOW)


def feed(rows, weight):
    part = pl.BlockSpec((512, 256), lambda i: (0, i))
    wide = jax.ShapeDtypeStruct((512, 512), WIDE)
    return pl.pallas_call(
        feed_kernel,
        grid=(2,),
        in_specs=[
            pl.BlockSpec((512, D), lambda i: (0, 0)),
            pl.BlockSpec((D, 256), lambda i: (0, i)),
            pl.BlockSpec((D, 256), lambda i: (0, i + 2)),
        ],
        out_specs=[part, part, part],
        out_shape=[wide, wide, jax.ShapeDtypeStruct((512, 512), LOW)],
        compiler_params=LIMIT,
        cost_estimate=estimate(2 * 512 * D * 1024, 8 * 1024 * 1024),
    )(rows, weight, weight)


def feed_out_kernel(act_ref, near_ref, far_ref, out_ref):
    act = act_ref[...]
    out_ref[:, :HALF] = contract(act, near_ref[...], 1, 0).astype(LOW)
    out_ref[:, HALF:] = contract(act, far_ref[...], 1, 0).astype(LOW)


def feed_out(act, near, far):
    whole = pl.BlockSpec((512, HALF), lambda i: (0, 0))
    return pl.pallas_call(
        feed_out_kernel,
        grid=(2,),
        in_specs=[pl.BlockSpec((256, 512), lambda i: (i, 0)), whole, whole],
        out_specs=pl.BlockSpec((256, D), lambda i: (i, 0)),
        out_shape=jax.ShapeDtypeStruct((512, D), LOW),
        compiler_params=LIMIT,
        cost_estimate=estimate(2 * 512 * 512 * D, 5 * 1024 * 1024),
    )(act, near, far)


def feed_back_kernel(rows_ref, near_ref, far_ref, gate_ref, upper_ref, out_ref):
    act_back = contract(rows_ref[:, :HALF], near_ref[...], 1, 1) + contract(
        rows_ref[:, HALF:], far_ref[...], 1, 1
    )
    gate, upper = gate_ref[...], upper_ref[...]
    sigmoid = jax.nn.sigmoid(gate)
    gate_back = act_back * upper * sigmoid * (1.0 + gate * (1.0 - sigmoid))
    out_ref[:, :512] = gate_back.astype(LOW)
    out_ref[:, 512:] = (act_back * (gate * sigmoid)).astype(LOW)


def feed_back(rows, near, far, gate, upper):
    whole = pl.BlockSpec((512, HALF), lambda i: (0, 0))
    part = pl.BlockSpec((256, 512), lambda i: (i, 0))
    return pl.pallas_call(
        feed_back_kernel,
        grid=(2,),
        in_specs=[pl.BlockSpec((256, D), lambda i: (i, 0)), whole, whole, part, part],
        out_specs=pl.BlockSpec((256, HALF), lambda i: (i, 0)),
        out_shape=jax.ShapeDtypeStruct((512, HALF), LOW),
        compiler_params=LIMIT,
        cost_estimate=estimate(2 * 512 * 512 * D, 7 * 1024 * 1024),
    )(rows, near, far, gate, upper)


def dense_kernel(arrived_ref, hidden_ref, cotangent_ref, scale_ref, copies_ref, out_ref, part_ref):
    dense = jnp.sum(arrived_ref[...].astype(WIDE), axis=0)
    rate = lax.rsqrt(jnp.mean(dense * dense, axis=1, keepdims=True) + EPSILON)
    hat = dense * rate
    scale = scale_ref[...]
    out_ref[...] = (hidden_ref[...] + hat * scale).astype(LOW)
    cotangent = cotangent_ref[...].astype(WIDE)
    part_ref[...] = jnp.sum(cotangent * hat, axis=0, keepdims=True)
    scaled = cotangent * scale
    dot = jnp.mean(scaled * hat, axis=1, keepdims=True)
    back = (rate * (scaled - hat * dot)).astype(LOW)
    for i in range(8):
        copies_ref[i * SUB : (i + 1) * SUB, :] = back


def dense_step(arrived, hidden, cotangent, scale):
    return pl.pallas_call(
        dense_kernel,
        out_shape=[
            jax.ShapeDtypeStruct((8 * SUB, D), LOW),
            jax.ShapeDtypeStruct((SUB, D), LOW),
            jax.ShapeDtypeStruct((1, D), WIDE),
        ],
        compiler_params=LIMIT,
        cost_estimate=estimate(20 * SUB * D, 6 * 1024 * 1024),
    )(arrived.reshape(8, SUB, D), hidden, cotangent, scale[None])


def hidden_kernel(arrived_ref, cotangent_ref, hat_ref, rate_ref, scale_ref, out_ref, low_ref, part_ref):
    hidden_back = cotangent_ref[...].astype(WIDE) + jnp.sum(arrived_ref[...].astype(WIDE), axis=0)
    hat = hat_ref[...]
    out_ref[...] = hidden_back
    part_ref[...] = jnp.sum(hidden_back * hat, axis=0, keepdims=True)
    scaled = hidden_back * scale_ref[...]
    dot = jnp.mean(scaled * hat, axis=1, keepdims=True)
    low_ref[...] = (rate_ref[...] * (scaled - hat * dot)).astype(LOW)


def hidden_step(arrived, cotangent, hat, rate, scale):
    return pl.pallas_call(
        hidden_kernel,
        out_shape=[
            jax.ShapeDtypeStruct((SUB, D), WIDE),
            jax.ShapeDtypeStruct((SUB, D), LOW),
            jax.ShapeDtypeStruct((1, D), WIDE),
        ],
        compiler_params=LIMIT,
        cost_estimate=estimate(20 * SUB * D, 4 * 1024 * 1024),
    )(arrived.reshape(8, SUB, D), cotangent, hat, rate, scale[None])


def local(
    tokens,
    w_heads,
    query_scale,
    key_scale,
    w_merge,
    attend_scale,
    w_gateup,
    w_down,
    dense_scale,
    cotangent,
):
    core = lax.axis_index("core")
    xh = lax.axis_index("xh")
    xl = lax.axis_index("xl")
    z = lax.axis_index("z")
    high = lax.axis_index("yh")

    shard = regroup(tokens)
    heads_in = w_heads.reshape(HALF, 3 * HEAD_DIM)
    gateup_in = w_gateup.reshape(HALF, 2 * 512)

    index = jnp.arange(512, dtype=jnp.int32)
    place = index // SUB * 128 + index % SUB
    places = (place + core * SUB, place + (1 - core) * SUB)
    tables = both(rope_tables, places)
    core_in = core.astype(jnp.int32)[None]

    copies = jnp.broadcast_to(shard[None], (8,) + shard.shape).reshape(8 * SUB, D)
    merge_in = after(copies, w_merge)
    merge_parts = (slice_near(merge_in), slice_far(merge_in))
    own, moved, (tables, gateup_in, merge) = beside(
        exchange,
        copies,
        (
            (slice_near, heads_in),
            (slice_far, heads_in),
        ),
        (tables, gateup_in, jnp.concatenate(merge_parts, axis=1)),
    )
    head_scales, width_scales = after(
        own, (jnp.stack([query_scale, key_scale]), jnp.stack([attend_scale, dense_scale]))
    )
    query_scale, key_scale = slice_near(head_scales)
    attend_scale, dense_scale = jnp.concatenate(
        [width_scales, move(width_scales, ("yl", "yh"), lambda l, h: (1 - l, 1 - h))], axis=1
    )
    heads = jnp.concatenate(moved, axis=0)
    merge = lax.all_gather(merge, ("core", "xl", "z"), axis=0, tiled=True)

    def squares(query, key):
        return jnp.stack([jnp.sum(query * query, axis=1), jnp.sum(key * key, axis=1)])

    def attend_whole(own):
        first, other = lax.optimization_barrier((contract(own, heads, 1, 0), to_core(own)))
        projected = (first, contract(other, heads, 1, 0))
        query_raw = both(lambda rows: rows[:, :HEAD_DIM], projected)
        key_raw = both(lambda rows: rows[:, HEAD_DIM : 2 * HEAD_DIM], projected)
        value_low = jnp.concatenate(
            both(lambda rows: rows[:, 2 * HEAD_DIM :].astype(LOW), projected), axis=0
        )
        powers, _ = group_sums(*both(squares, query_raw, key_raw))
        rates = both(lambda rows: lax.rsqrt(rows / D + EPSILON), powers)
        query_rate = both(lambda rows: rows[0][:, None], rates)
        key_rate = both(lambda rows: rows[1][:, None], rates)
        query_hat = both(lambda raw, rate: raw * rate, query_raw, query_rate)
        key_hat = both(lambda raw, rate: raw * rate, key_raw, key_rate)
        query_low = jnp.concatenate(
            both(
                lambda hat, table: rotate(hat * query_scale, *table).astype(LOW), query_hat, tables
            ),
            axis=0,
        )
        key_low = jnp.concatenate(
            both(lambda hat, table: rotate(hat * key_scale, *table).astype(LOW), key_hat, tables),
            axis=0,
        )

        mixed_low, log_total = attend(core_in, query_low, key_low, value_low)
        attended = contract(to_owners(mixed_low[:512], mixed_low[512:]), merge, 1, 0)
        return (
            (own, other),
            (query_rate, key_rate, query_hat, key_hat),
            (query_low, key_low, value_low),
            mixed_low,
            log_total,
            attended,
        )

    (whole, norms, lows, mixed_low, log_total, attended), gateup_parts, _ = beside(
        attend_whole, own, ((slice_near, gateup_in), (slice_far, gateup_in))
    )
    query_rate, key_rate, query_hat, key_hat = norms
    query_low, key_low, value_low = lows
    attend_rate = lax.rsqrt(jnp.mean(attended * attended, axis=1, keepdims=True) + EPSILON)
    attend_hat = attended * attend_rate
    hidden = shard.astype(WIDE) + attend_hat * attend_scale

    copies = jnp.broadcast_to(hidden.astype(LOW)[None], (8, SUB, D)).reshape(8 * SUB, D)
    own, down_parts, gateup_w = beside(
        exchange,
        copies,
        ((slice_near, w_down), (slice_far, w_down)),
        jnp.concatenate(gateup_parts, axis=0),
    )

    first, other = lax.optimization_barrier((feed(own, gateup_w), to_core(own)))
    fed = (first, feed(other, gateup_w))
    hidden_whole = (own, other)
    act_low = both(lambda parts: parts[2], fed)
    arrived, (grad_out,) = scatter_parts(
        lambda i: feed_out(act_low[i], *down_parts), ((regroup, cotangent),)
    )
    copies, output, dense_part = dense_step(arrived, hidden, grad_out, dense_scale)

    own, (output,), _ = beside(exchange, copies, ((ungroup, output),))

    def back_through(i, rows):
        return feed_back(rows, *down_parts, fed[i][0], fed[i][1])

    first, other = lax.optimization_barrier((back_through(0, own), to_core(own)))
    dense_back = (own, other)
    gateup_back_low = (first, back_through(1, other))

    def weight_grad(left, right):
        return (contract(left[0], right[0], 0, 0) + contract(left[1], right[1], 0, 0)).astype(LOW)

    grad_down = [weight_grad(act_low, rows) for rows in halves(dense_back)]
    arrived = to_core(contract(gateup_back_low[1], gateup_w, 1, 1).astype(LOW))
    first, arrived = lax.optimization_barrier(
        (contract(gateup_back_low[0], gateup_w, 1, 1).astype(LOW), arrived)
    )
    mine, *grad_down = lax.optimization_barrier((add_low(first, arrived), *grad_down))
    down_grads = (give_near(grad_down[0]), slice_far(grad_down[1]))
    arrived, grad_gateup = lax.optimization_barrier(
        (
            exchange(mine),
            tuple(weight_grad(rows, gateup_back_low) for rows in halves(hidden_whole)),
        )
    )
    hidden_back, attended_back_low, attend_part = hidden_step(
        arrived, grad_out, attend_hat, attend_rate, attend_scale
    )
    attended_back = lax.all_gather(attended_back_low, ("core", "xl", "z"), axis=0, tiled=True)
    mixed_whole = jnp.concatenate(by_core(mixed_low[:512], mixed_low[512:]), axis=0)

    def products(query, query_hat, key, key_hat):
        return jnp.stack([jnp.sum(query * query_hat, axis=1), jnp.sum(key * key_hat, axis=1)])

    def through_norm(rate, scaled, hat, dot):
        return rate * (scaled - hat * dot[:, None])

    def column_sum(first, second):
        return sum(both(lambda a, b: jnp.sum(a * b, axis=0), first, second))

    def attend_whole_back(rows, gateup_parts, down_grads):
        attended_back_low, attend_part = rows
        mixed_back, down_grads = lax.optimization_barrier(
            (contract(attended_back_low, merge, 1, 1), down_grads)
        )
        down_halves = halves_of_sibling(down_grads)
        mixed_back_low = to_heads(mixed_back.astype(LOW))
        mixed_back_low = jnp.concatenate(by_core(mixed_back_low[:512], mixed_back_low[512:]))
        (query_turned, key_turned, value_back), gateup_parts = lax.optimization_barrier(
            (
                attend_back(core_in, query_low, key_low, value_low, log_total, mixed_back_low),
                gateup_parts,
            )
        )
        query_norm_back = both(
            lambda rows, table: rotate_back(rows, *table),
            (query_turned[:512], query_turned[512:]),
            tables,
        )
        value_back = (value_back[:512], value_back[512:])
        key_norm_back = both(
            lambda rows, table: rotate_back(rows, *table),
            (key_turned[:512], key_turned[512:]),
            tables,
        )
        query_scaled = both(lambda rows: rows * query_scale, query_norm_back)
        key_scaled = both(lambda rows: rows * key_scale, key_norm_back)
        parts = jnp.concatenate(
            [
                column_sum(query_norm_back, query_hat)[None],
                column_sum(key_norm_back, key_hat)[None],
                attend_part.reshape(16, 128),
                dense_part.reshape(16, 128),
            ],
            axis=0,
        )
        dots, parts = group_sums(
            *both(products, query_scaled, query_hat, key_scaled, key_hat), parts
        )
        query_back = both(
            through_norm, query_rate, query_scaled, query_hat, (dots[0][0] / D, dots[1][0] / D)
        )
        key_back = both(
            through_norm, key_rate, key_scaled, key_hat, (dots[0][1] / D, dots[1][1] / D)
        )
        back = both(
            lambda *parts: jnp.concatenate(parts, axis=1).astype(LOW),
            query_back,
            key_back,
            value_back,
        )
        return back, parts, half_of_both(*gateup_parts), down_halves

    rows_in, ride_in = lax.optimization_barrier(
        (
            (attended_back_low, attend_part),
            grad_gateup,
        )
    )
    gateup_parts = (give_near(ride_in[0]), slice_far(ride_in[1]))
    projected_back_low, parts, gateup_half, down_halves = lax.optimization_barrier(
        attend_whole_back(rows_in, gateup_parts, down_grads)
    )
    grad_heads = [weight_grad(projected_back_low, rows) for rows in halves(whole)]
    heads_parts = (give_near(grad_heads[0]), slice_far(grad_heads[1]))

    first, second = after(grad_heads, projected_back_low)
    arrived = to_core(contract(second, heads, 1, 1).astype(LOW))
    first, arrived = lax.optimization_barrier((contract(first, heads, 1, 1).astype(LOW), arrived))
    mine = add_low(first, arrived)
    attended_back, down_halves, parts = after(mine, (attended_back, down_halves, parts))
    grad_merge = [
        contract(mixed_whole, rows, 0, 0).astype(LOW)
        for rows in (attended_back[:, :HALF], attended_back[:, HALF:])
    ]

    rows = by_slice(parts[:, :2])
    rows = jnp.moveaxis(rows, 1, 0).reshape(4, HALF)
    width = jnp.sum(parts[:, 2:], axis=0).reshape(2, 2, HALF)
    width = jnp.where(high == 0, width, width[:, ::-1]).reshape(4, HALF)
    gains = jnp.concatenate([rows, width, jnp.zeros((24, HALF), WIDE)], axis=0).astype(LOW)
    merge_near = jnp.concatenate([grad_merge[0], gains], axis=0)
    merge_far = jnp.concatenate([grad_merge[1], gains], axis=0)

    merge_parts = (give_near(merge_near), slice_far(merge_far))
    small_parts = both(lambda *parts: jnp.concatenate(parts, axis=0), heads_parts, merge_parts)
    small_parts, gateup_arrived = lax.optimization_barrier(
        (small_parts, to_sibling(gateup_half))
    )
    arrived, grad_down, small_half = lax.optimization_barrier(
        (
            exchange(mine),
            whole_of_half(*down_halves).astype(WIDE),
            half_of_both(*small_parts),
        )
    )
    tokens_back = jnp.sum(arrived.reshape(8, SUB, D).astype(WIDE), axis=0)
    small_arrived, grad_gateup, grad_tokens = lax.optimization_barrier(
        (
            to_sibling(small_half),
            spread_gateup(whole_of_half(gateup_half, gateup_arrived)),
            ungroup((hidden_back + tokens_back).astype(LOW)),
        )
    )
    small = whole_of_half(small_half, small_arrived)
    grad_heads = spread_heads(small)
    grad_merge = small[3 * HEAD_DIM : 4 * HEAD_DIM].astype(WIDE)
    gains = small[4 * HEAD_DIM : 4 * HEAD_DIM + 8].astype(WIDE).reshape(4, D)
    return (
        output,
        grad_tokens,
        grad_heads,
        grad_merge,
        grad_gateup,
        grad_down,
        gains[0],
        gains[1],
        gains[2],
        gains[3],
    )


def solution(mesh):
    fine = Mesh(mesh.devices.reshape(tuple(SIZES[name] for name in NAMES)), NAMES)
    dp, row, col = ("yl", "core"), ("xh", "xl", "z"), "yh"
    in_specs = (
        P(dp + row, col),
        P(col, None, row),
        P(row),
        P(row),
        P(row, col),
        P(col),
        P(col, None, row),
        P(row, col),
        P(col),
        P(dp + row, col),
    )
    out_specs = (
        P(dp + row, col),
        P(dp + row, col),
        P(col, None, row),
        P(row, col),
        P(col, None, row),
        P(row, col),
        P(),
        P(),
        P(),
        P(),
    )
    return jax.shard_map(local, mesh=fine, in_specs=in_specs, out_specs=out_specs, check_vma=False)
```

```python
import itertools

import jax
import jax.numpy as jnp
from jax import lax
from jax.experimental import pallas as pl
from jax.experimental.pallas import tpu as pltpu
from jax.sharding import Mesh
from jax.sharding import PartitionSpec as P

D = 2048
HEAD_DIM = 128
SEQ_LEN = 1024
HALF = 1024
SUB = 64
EPSILON = 1e-06
THETA = 500000.0
NEGATIVE = -1e30

LOW = jnp.bfloat16
WIDE = jnp.float32

NAMES = ("yl", "core", "xh", "xl", "z", "yh")
SIZES = {"yl": 2, "core": 2, "xh": 2, "xl": 2, "z": 4, "yh": 2}


def contract(left, right, left_dim, right_dim):
    return lax.dot_general(
        left, right, (((left_dim,), (right_dim,)), ((), ())), preferred_element_type=WIDE
    )


def pairs_of(axes, target):
    sizes = [SIZES[name] for name in axes]

    def flat(place):
        index = 0
        for value, size in zip(place, sizes):
            index = index * size + value
        return index

    return [
        (flat(place), flat(target(*place)))
        for place in itertools.product(*[range(size) for size in sizes])
    ]


def move(value, axes, target):
    return lax.ppermute(value, axes, pairs_of(axes, target))


def to_core(value):
    return move(value, ("core",), lambda c: (1 - c,))


def to_sibling(value):
    return move(value, ("yl",), lambda a: (1 - a,))


def slice_near(value):
    return move(
        value,
        ("core", "xh", "xl"),
        lambda c, a, b: (c, 1 - a, 1 - b) if c == a else (1 - c, a, b),
    )


def give_near(value):
    return move(
        value,
        ("core", "xh", "xl"),
        lambda c, a, b: (1 - c, a, b) if c == a else (c, 1 - a, 1 - b),
    )


def slice_far(value):
    return move(
        value,
        ("yl", "core", "xh", "xl", "yh"),
        lambda l, c, a, b, h: (1 - l, c, a, b, 1 - h)
        if c == a
        else (1 - l, 1 - c, 1 - a, 1 - b, 1 - h),
    )


def after(value, arrays):
    return lax.optimization_barrier((value, arrays))[1]


def beside(function, value, rides, work=()):
    value, arrays = lax.optimization_barrier((value, tuple(array for _, array in rides)))
    moved = tuple(ride(array) for (ride, _), array in zip(rides, arrays))
    return lax.optimization_barrier((function(value), moved, work))


def exchange(rows):
    return lax.all_to_all(rows, ("xl", "z"), 0, 0, tiled=True)


def scatter_parts(function, rides=()):
    arrived = to_core(function(1))
    own, arrived = lax.optimization_barrier((function(0), arrived))
    arrived, moved, _ = beside(exchange, add_low(own, arrived), rides)
    return arrived, moved


def by_core(first, second):
    own_first = lax.axis_index("core") == 0
    return jnp.where(own_first, first, second), jnp.where(own_first, second, first)


def group_copies(rows):
    copies = jnp.broadcast_to(rows[None], (16,) + rows.shape).reshape(-1, 128)
    arrived = lax.all_to_all(copies, ("core", "xl", "z"), 0, 0, tiled=True)
    return arrived.reshape((16,) + rows.shape)


def group_sums(own, other, more=None):
    whole = jnp.concatenate(by_core(own, other), axis=0).reshape(16, 128)
    if more is not None:
        whole = jnp.concatenate([whole, more], axis=0)
    arrived = group_copies(whole)
    total = jnp.sum(arrived[:, :16], axis=0).reshape(2, 2, 512)
    return by_core(total[0], total[1]), arrived[:, 16:]


def by_slice(blocks):
    view = blocks.reshape((2, 2, 4) + blocks.shape[1:])
    straight = jnp.arange(2) == lax.axis_index("xh")
    straight = straight.reshape((2,) + (1,) * (view.ndim - 2))
    first = jnp.where(straight, view[:, 0], view[:, 1])
    second = jnp.where(straight, view[:, 1], view[:, 0])
    return jnp.stack([first, second], axis=1).reshape(blocks.shape)


def to_owners(own, other):
    blocks = jnp.concatenate(by_core(own, other), axis=0)
    arrived = lax.all_to_all(blocks, ("core", "xl", "z"), 0, 0, tiled=True)
    return jnp.swapaxes(arrived.reshape(16, SUB, HEAD_DIM), 0, 1).reshape(SUB, D)


def to_heads(rows):
    blocks = jnp.swapaxes(rows.reshape(SUB, 16, HEAD_DIM), 0, 1).reshape(16 * SUB, HEAD_DIM)
    return lax.all_to_all(blocks, ("core", "xl", "z"), 0, 0, tiled=True)


def both(function, *pairs):
    return tuple(function(*items) for items in zip(*pairs))


def halves(pair):
    return tuple(rows[:, :HALF] for rows in pair), tuple(rows[:, HALF:] for rows in pair)


def add_low(first, *others):
    total = first.astype(WIDE)
    for other in others:
        total = total + other.astype(WIDE)
    return total.astype(LOW)


def regroup(block):
    core = lax.axis_index("core")
    high = lax.axis_index("yh")
    lower, upper = block[:SUB], block[SUB:]
    parts = []
    for j in (0, 1):
        piece = jnp.where((high ^ j) == 0, lower, upper)
        parts.append(move(piece, ("core", "yh"), lambda c, h: (h ^ j, c)))
    same = core == high
    return jnp.concatenate(
        [jnp.where(same, parts[0], parts[1]), jnp.where(same, parts[1], parts[0])], axis=1
    )


def ungroup(block):
    core = lax.axis_index("core")
    high = lax.axis_index("yh")
    near, far = block[:, :HALF], block[:, HALF:]
    parts = []
    for j in (0, 1):
        piece = jnp.where((core ^ j) == high, near, far)
        parts.append(move(piece, ("core", "yh"), lambda c, h: (h, c ^ j)))
    first = high == 0
    return jnp.concatenate(
        [jnp.where(first, parts[0], parts[1]), jnp.where(first, parts[1], parts[0])], axis=0
    )


def half_of_both(arrived_near, arrived_far):
    part = arrived_near.astype(WIDE) + arrived_far.astype(WIDE)
    rows = part.shape[0] // 2
    core = lax.axis_index("core")
    lower, upper = part[:rows], part[rows:]
    keep = jnp.where(core == 0, lower, upper)
    give = jnp.where(core == 0, upper, lower).astype(LOW)
    return (keep + to_core(give).astype(WIDE)).astype(LOW)


def halves_of_sibling(parts):
    half = half_of_both(*parts)
    return half, to_sibling(half)


def whole_of_half(half, arrived):
    core = lax.axis_index("core")
    half = add_low(half, arrived)
    other = to_core(half)
    return jnp.concatenate(
        [jnp.where(core == 0, half, other), jnp.where(core == 0, other, half)], axis=0
    )


def rope_tables(place):
    pairs = HEAD_DIM // 2
    freq = THETA ** (-(jnp.arange(pairs, dtype=WIDE) * (2.0 / HEAD_DIM)))
    angle = place.astype(WIDE)[:, None] * freq[None, :]
    cosine = jnp.concatenate([jnp.cos(angle), jnp.cos(angle)], axis=1)
    sine = jnp.concatenate([jnp.sin(angle), jnp.sin(angle)], axis=1)
    return (cosine, sine)


def rotate(values, cosine, sine):
    pairs = HEAD_DIM // 2
    turned = jnp.concatenate([-values[:, pairs:], values[:, :pairs]], axis=1)
    return values * cosine + turned * sine


def rotate_back(grad, cosine, sine):
    pairs = HEAD_DIM // 2
    scaled = grad * sine
    turned = jnp.concatenate([scaled[:, pairs:], -scaled[:, :pairs]], axis=1)
    return grad * cosine + turned


ROWS = 256
SCALE = HEAD_DIM ** (-0.5)


def places_of(index, core):
    block, row = (index % 512) // SUB, index % SUB
    return block * 128 + jnp.where(index < 512, core, 1 - core) * SUB + row


def block_scores(core_ref, query, key):
    first = pl.program_id(0) * ROWS
    query_index = first + lax.broadcasted_iota(jnp.int32, (ROWS, 1), 0)
    key_index = lax.broadcasted_iota(jnp.int32, (1, SEQ_LEN), 1)
    core = core_ref[0]
    allowed = places_of(key_index, core) <= places_of(query_index, core)
    return jnp.where(allowed, contract(query, key, 1, 1) * SCALE, NEGATIVE)


def attend_kernel(core_ref, query_ref, key_ref, value_ref, mixed_ref, total_ref):
    scores = block_scores(core_ref, query_ref[...], key_ref[...])
    top = jnp.max(scores, axis=1, keepdims=True)
    shifted = jnp.exp(scores - top)
    total = jnp.sum(shifted, axis=1, keepdims=True)
    probs_low = (shifted * (1.0 / total)).astype(LOW)
    mixed_ref[...] = contract(probs_low, value_ref[...], 1, 0).astype(LOW)
    total_ref[...] = jnp.broadcast_to(top + jnp.log(total), total_ref.shape)


def attend_back_kernel(
    core_ref,
    query_ref,
    key_ref,
    value_ref,
    total_ref,
    mixed_back_ref,
    query_out,
    key_out,
    value_out,
):
    query, key, mixed_back = query_ref[...], key_ref[...], mixed_back_ref[...]
    probs = jnp.exp(block_scores(core_ref, query, key) - total_ref[...][:, :1])
    probs_back = contract(mixed_back, value_ref[...], 1, 1)
    row_dot = jnp.sum(probs_back * probs, axis=1, keepdims=True)
    scores_back = (probs * (probs_back - row_dot)).astype(LOW)
    query_out[...] = contract(scores_back, key, 1, 0) * SCALE
    key_part = contract(scores_back, query, 0, 0) * SCALE
    value_part = contract(probs.astype(LOW), mixed_back, 0, 0)

    @pl.when(pl.program_id(0) == 0)
    def _():
        key_out[...] = key_part
        value_out[...] = value_part

    @pl.when(pl.program_id(0) > 0)
    def _():
        key_out[...] += key_part
        value_out[...] += value_part


def row_spec():
    return pl.BlockSpec((ROWS, HEAD_DIM), lambda i: (i, 0))


def whole_spec():
    return pl.BlockSpec((SEQ_LEN, HEAD_DIM), lambda i: (0, 0))


def core_spec():
    return pl.BlockSpec(memory_space=pltpu.SMEM)


def head_call(kernel, in_specs, out_specs, out_types):
    return pl.pallas_call(
        kernel,
        grid=(SEQ_LEN // ROWS,),
        in_specs=in_specs,
        out_specs=out_specs,
        out_shape=[jax.ShapeDtypeStruct((SEQ_LEN, HEAD_DIM), kind) for kind in out_types],
        compiler_params=pltpu.CompilerParams(vmem_limit_bytes=32 * 1024 * 1024),
        cost_estimate=pl.CostEstimate(flops=0, bytes_accessed=0, transcendentals=0),
    )


def attend(core, query, key, value):
    return head_call(
        attend_kernel,
        [core_spec(), row_spec(), whole_spec(), whole_spec()],
        [row_spec(), row_spec()],
        [LOW, WIDE],
    )(core, query, key, value)


def attend_back(core, query, key, value, total, mixed_back):
    return head_call(
        attend_back_kernel,
        [core_spec(), row_spec(), whole_spec(), whole_spec(), row_spec(), row_spec()],
        [row_spec(), whole_spec(), whole_spec()],
        [WIDE, WIDE, WIDE],
    )(core, query, key, value, total, mixed_back)


def spread_kernel(rows_ref, heads_ref):
    for i in range(3):
        part = rows_ref[i * HEAD_DIM : (i + 1) * HEAD_DIM, :]
        heads_ref[:, i, :] = jnp.transpose(part.astype(WIDE))


def spread_heads(rows):
    return pl.pallas_call(
        spread_kernel,
        grid=(2,),
        in_specs=[pl.BlockSpec((3 * HEAD_DIM, 512), lambda i: (0, i))],
        out_specs=pl.BlockSpec((512, 3, HEAD_DIM), lambda i: (i, 0, 0)),
        out_shape=jax.ShapeDtypeStruct((HALF, 3, HEAD_DIM), WIDE),
        compiler_params=pltpu.CompilerParams(vmem_limit_bytes=32 * 1024 * 1024),
    )(rows)


def spread_gateup_kernel(rows_ref, gateup_ref):
    for i in range(2):
        gateup_ref[:, i, :] = rows_ref[:, i * 512 : (i + 1) * 512].astype(WIDE)


def spread_gateup(rows):
    return pl.pallas_call(
        spread_gateup_kernel,
        grid=(4,),
        in_specs=[pl.BlockSpec((256, HALF), lambda i: (i, 0))],
        out_specs=pl.BlockSpec((256, 2, 512), lambda i: (i, 0, 0)),
        out_shape=jax.ShapeDtypeStruct((HALF, 2, 512), WIDE),
        compiler_params=pltpu.CompilerParams(vmem_limit_bytes=32 * 1024 * 1024),
    )(rows)


LIMIT = pltpu.CompilerParams(vmem_limit_bytes=40 * 1024 * 1024)


def estimate(flops, moved):
    return pl.CostEstimate(flops=flops, bytes_accessed=moved, transcendentals=0)


def feed_kernel(rows_ref, gate_w_ref, upper_w_ref, gate_ref, upper_ref, act_ref):
    rows = rows_ref[...]
    gate = contract(rows, gate_w_ref[...], 1, 0)
    upper = contract(rows, upper_w_ref[...], 1, 0)
    gate_ref[...] = gate
    upper_ref[...] = upper
    act_ref[...] = (gate * jax.nn.sigmoid(gate) * upper).astype(LOW)


def feed(rows, weight):
    part = pl.BlockSpec((512, 256), lambda i: (0, i))
    wide = jax.ShapeDtypeStruct((512, 512), WIDE)
    return pl.pallas_call(
        feed_kernel,
        grid=(2,),
        in_specs=[
            pl.BlockSpec((512, D), lambda i: (0, 0)),
            pl.BlockSpec((D, 256), lambda i: (0, i)),
            pl.BlockSpec((D, 256), lambda i: (0, i + 2)),
        ],
        out_specs=[part, part, part],
        out_shape=[wide, wide, jax.ShapeDtypeStruct((512, 512), LOW)],
        compiler_params=LIMIT,
        cost_estimate=estimate(2 * 512 * D * 1024, 8 * 1024 * 1024),
    )(rows, weight, weight)


def feed_out_kernel(act_ref, near_ref, far_ref, out_ref):
    act = act_ref[...]
    out_ref[:, :HALF] = contract(act, near_ref[...], 1, 0).astype(LOW)
    out_ref[:, HALF:] = contract(act, far_ref[...], 1, 0).astype(LOW)


def feed_out(act, near, far):
    whole = pl.BlockSpec((512, HALF), lambda i: (0, 0))
    return pl.pallas_call(
        feed_out_kernel,
        grid=(2,),
        in_specs=[pl.BlockSpec((256, 512), lambda i: (i, 0)), whole, whole],
        out_specs=pl.BlockSpec((256, D), lambda i: (i, 0)),
        out_shape=jax.ShapeDtypeStruct((512, D), LOW),
        compiler_params=LIMIT,
        cost_estimate=estimate(2 * 512 * 512 * D, 5 * 1024 * 1024),
    )(act, near, far)


def feed_back_kernel(rows_ref, near_ref, far_ref, gate_ref, upper_ref, out_ref):
    act_back = contract(rows_ref[:, :HALF], near_ref[...], 1, 1) + contract(
        rows_ref[:, HALF:], far_ref[...], 1, 1
    )
    gate, upper = gate_ref[...], upper_ref[...]
    sigmoid = jax.nn.sigmoid(gate)
    gate_back = act_back * upper * sigmoid * (1.0 + gate * (1.0 - sigmoid))
    out_ref[:, :512] = gate_back.astype(LOW)
    out_ref[:, 512:] = (act_back * (gate * sigmoid)).astype(LOW)


def feed_back(rows, near, far, gate, upper):
    whole = pl.BlockSpec((512, HALF), lambda i: (0, 0))
    part = pl.BlockSpec((256, 512), lambda i: (i, 0))
    return pl.pallas_call(
        feed_back_kernel,
        grid=(2,),
        in_specs=[pl.BlockSpec((256, D), lambda i: (i, 0)), whole, whole, part, part],
        out_specs=pl.BlockSpec((256, HALF), lambda i: (i, 0)),
        out_shape=jax.ShapeDtypeStruct((512, HALF), LOW),
        compiler_params=LIMIT,
        cost_estimate=estimate(2 * 512 * 512 * D, 7 * 1024 * 1024),
    )(rows, near, far, gate, upper)


def dense_kernel(arrived_ref, hidden_ref, cotangent_ref, scale_ref, copies_ref, out_ref, part_ref):
    dense = jnp.sum(arrived_ref[...].astype(WIDE), axis=0)
    rate = lax.rsqrt(jnp.mean(dense * dense, axis=1, keepdims=True) + EPSILON)
    hat = dense * rate
    scale = scale_ref[...]
    out_ref[...] = (hidden_ref[...] + hat * scale).astype(LOW)
    cotangent = cotangent_ref[...].astype(WIDE)
    part_ref[...] = jnp.sum(cotangent * hat, axis=0, keepdims=True)
    scaled = cotangent * scale
    dot = jnp.mean(scaled * hat, axis=1, keepdims=True)
    back = (rate * (scaled - hat * dot)).astype(LOW)
    for i in range(8):
        copies_ref[i * SUB : (i + 1) * SUB, :] = back


def dense_step(arrived, hidden, cotangent, scale):
    return pl.pallas_call(
        dense_kernel,
        out_shape=[
            jax.ShapeDtypeStruct((8 * SUB, D), LOW),
            jax.ShapeDtypeStruct((SUB, D), LOW),
            jax.ShapeDtypeStruct((1, D), WIDE),
        ],
        compiler_params=LIMIT,
        cost_estimate=estimate(20 * SUB * D, 6 * 1024 * 1024),
    )(arrived.reshape(8, SUB, D), hidden, cotangent, scale[None])


def hidden_kernel(arrived_ref, cotangent_ref, hat_ref, rate_ref, scale_ref, out_ref, low_ref, part_ref):
    hidden_back = cotangent_ref[...].astype(WIDE) + jnp.sum(arrived_ref[...].astype(WIDE), axis=0)
    hat = hat_ref[...]
    out_ref[...] = hidden_back
    part_ref[...] = jnp.sum(hidden_back * hat, axis=0, keepdims=True)
    scaled = hidden_back * scale_ref[...]
    dot = jnp.mean(scaled * hat, axis=1, keepdims=True)
    low_ref[...] = (rate_ref[...] * (scaled - hat * dot)).astype(LOW)


def hidden_step(arrived, cotangent, hat, rate, scale):
    return pl.pallas_call(
        hidden_kernel,
        out_shape=[
            jax.ShapeDtypeStruct((SUB, D), WIDE),
            jax.ShapeDtypeStruct((SUB, D), LOW),
            jax.ShapeDtypeStruct((1, D), WIDE),
        ],
        compiler_params=LIMIT,
        cost_estimate=estimate(20 * SUB * D, 4 * 1024 * 1024),
    )(arrived.reshape(8, SUB, D), cotangent, hat, rate, scale[None])


def local(
    tokens,
    w_heads,
    query_scale,
    key_scale,
    w_merge,
    attend_scale,
    w_gateup,
    w_down,
    dense_scale,
    cotangent,
):
    core = lax.axis_index("core")
    xh = lax.axis_index("xh")
    xl = lax.axis_index("xl")
    z = lax.axis_index("z")
    high = lax.axis_index("yh")

    shard = regroup(tokens)
    heads_in = w_heads.reshape(HALF, 3 * HEAD_DIM)
    gateup_in = w_gateup.reshape(HALF, 2 * 512)

    index = jnp.arange(512, dtype=jnp.int32)
    place = index // SUB * 128 + index % SUB
    places = (place + core * SUB, place + (1 - core) * SUB)
    tables = both(rope_tables, places)
    core_in = core.astype(jnp.int32)[None]

    copies = jnp.broadcast_to(shard[None], (8,) + shard.shape).reshape(8 * SUB, D)
    merge_parts = (slice_near(w_merge), slice_far(w_merge))
    own, moved, (tables, gateup_in, merge) = beside(
        exchange,
        copies,
        (
            (slice_near, heads_in),
            (slice_far, heads_in),
        ),
        (tables, gateup_in, jnp.concatenate(merge_parts, axis=1)),
    )
    head_scales, width_scales = after(
        own, (jnp.stack([query_scale, key_scale]), jnp.stack([attend_scale, dense_scale]))
    )
    query_scale, key_scale = slice_near(head_scales)
    attend_scale, dense_scale = jnp.concatenate(
        [width_scales, move(width_scales, ("yl", "yh"), lambda l, h: (1 - l, 1 - h))], axis=1
    )
    heads = jnp.concatenate(moved, axis=0)
    merge = lax.all_gather(merge, ("core", "xl", "z"), axis=0, tiled=True)

    def squares(query, key):
        return jnp.stack([jnp.sum(query * query, axis=1), jnp.sum(key * key, axis=1)])

    def attend_whole(own):
        first, other = lax.optimization_barrier((contract(own, heads, 1, 0), to_core(own)))
        projected = (first, contract(other, heads, 1, 0))
        query_raw = both(lambda rows: rows[:, :HEAD_DIM], projected)
        key_raw = both(lambda rows: rows[:, HEAD_DIM : 2 * HEAD_DIM], projected)
        value_low = jnp.concatenate(
            both(lambda rows: rows[:, 2 * HEAD_DIM :].astype(LOW), projected), axis=0
        )
        powers, _ = group_sums(*both(squares, query_raw, key_raw))
        rates = both(lambda rows: lax.rsqrt(rows / D + EPSILON), powers)
        query_rate = both(lambda rows: rows[0][:, None], rates)
        key_rate = both(lambda rows: rows[1][:, None], rates)
        query_hat = both(lambda raw, rate: raw * rate, query_raw, query_rate)
        key_hat = both(lambda raw, rate: raw * rate, key_raw, key_rate)
        query_low = jnp.concatenate(
            both(
                lambda hat, table: rotate(hat * query_scale, *table).astype(LOW), query_hat, tables
            ),
            axis=0,
        )
        key_low = jnp.concatenate(
            both(lambda hat, table: rotate(hat * key_scale, *table).astype(LOW), key_hat, tables),
            axis=0,
        )

        mixed_low, log_total = attend(core_in, query_low, key_low, value_low)
        attended = contract(to_owners(mixed_low[:512], mixed_low[512:]), merge, 1, 0)
        return (
            (own, other),
            (query_rate, key_rate, query_hat, key_hat),
            (query_low, key_low, value_low),
            mixed_low,
            log_total,
            attended,
        )

    (whole, norms, lows, mixed_low, log_total, attended), gateup_parts, _ = beside(
        attend_whole, own, ((slice_near, gateup_in), (slice_far, gateup_in))
    )
    query_rate, key_rate, query_hat, key_hat = norms
    query_low, key_low, value_low = lows
    attend_rate = lax.rsqrt(jnp.mean(attended * attended, axis=1, keepdims=True) + EPSILON)
    attend_hat = attended * attend_rate
    hidden = shard.astype(WIDE) + attend_hat * attend_scale

    copies = jnp.broadcast_to(hidden.astype(LOW)[None], (8, SUB, D)).reshape(8 * SUB, D)
    own, down_parts, gateup_w = beside(
        exchange,
        copies,
        ((slice_near, w_down), (slice_far, w_down)),
        jnp.concatenate(gateup_parts, axis=0),
    )

    first, other = lax.optimization_barrier((feed(own, gateup_w), to_core(own)))
    fed = (first, feed(other, gateup_w))
    hidden_whole = (own, other)
    act_low = both(lambda parts: parts[2], fed)
    arrived, (grad_out,) = scatter_parts(
        lambda i: feed_out(act_low[i], *down_parts), ((regroup, cotangent),)
    )
    copies, output, dense_part = dense_step(arrived, hidden, grad_out, dense_scale)

    own, (output,), _ = beside(exchange, copies, ((ungroup, output),))

    def back_through(i, rows):
        return feed_back(rows, *down_parts, fed[i][0], fed[i][1])

    first, other = lax.optimization_barrier((back_through(0, own), to_core(own)))
    dense_back = (own, other)
    gateup_back_low = (first, back_through(1, other))

    def weight_grad(left, right):
        return (contract(left[0], right[0], 0, 0) + contract(left[1], right[1], 0, 0)).astype(LOW)

    grad_down = [weight_grad(act_low, rows) for rows in halves(dense_back)]
    arrived = to_core(contract(gateup_back_low[1], gateup_w, 1, 1).astype(LOW))
    first, arrived = lax.optimization_barrier(
        (contract(gateup_back_low[0], gateup_w, 1, 1).astype(LOW), arrived)
    )
    mine, *grad_down = lax.optimization_barrier((add_low(first, arrived), *grad_down))
    down_grads = (give_near(grad_down[0]), slice_far(grad_down[1]))
    arrived, grad_gateup = lax.optimization_barrier(
        (
            exchange(mine),
            tuple(weight_grad(rows, gateup_back_low) for rows in halves(hidden_whole)),
        )
    )
    hidden_back, attended_back_low, attend_part = hidden_step(
        arrived, grad_out, attend_hat, attend_rate, attend_scale
    )
    attended_back = lax.all_gather(attended_back_low, ("core", "xl", "z"), axis=0, tiled=True)
    mixed_whole = jnp.concatenate(by_core(mixed_low[:512], mixed_low[512:]), axis=0)

    def products(query, query_hat, key, key_hat):
        return jnp.stack([jnp.sum(query * query_hat, axis=1), jnp.sum(key * key_hat, axis=1)])

    def through_norm(rate, scaled, hat, dot):
        return rate * (scaled - hat * dot[:, None])

    def column_sum(first, second):
        return sum(both(lambda a, b: jnp.sum(a * b, axis=0), first, second))

    def attend_whole_back(rows, gateup_parts, down_grads):
        attended_back_low, attend_part = rows
        mixed_back, down_grads = lax.optimization_barrier(
            (contract(attended_back_low, merge, 1, 1), down_grads)
        )
        down_halves = halves_of_sibling(down_grads)
        mixed_back_low = to_heads(mixed_back.astype(LOW))
        mixed_back_low = jnp.concatenate(by_core(mixed_back_low[:512], mixed_back_low[512:]))
        (query_turned, key_turned, value_back), gateup_parts = lax.optimization_barrier(
            (
                attend_back(core_in, query_low, key_low, value_low, log_total, mixed_back_low),
                gateup_parts,
            )
        )
        query_norm_back = both(
            lambda rows, table: rotate_back(rows, *table),
            (query_turned[:512], query_turned[512:]),
            tables,
        )
        value_back = (value_back[:512], value_back[512:])
        key_norm_back = both(
            lambda rows, table: rotate_back(rows, *table),
            (key_turned[:512], key_turned[512:]),
            tables,
        )
        query_scaled = both(lambda rows: rows * query_scale, query_norm_back)
        key_scaled = both(lambda rows: rows * key_scale, key_norm_back)
        parts = jnp.concatenate(
            [
                column_sum(query_norm_back, query_hat)[None],
                column_sum(key_norm_back, key_hat)[None],
                attend_part.reshape(16, 128),
                dense_part.reshape(16, 128),
            ],
            axis=0,
        )
        dots, parts = group_sums(
            *both(products, query_scaled, query_hat, key_scaled, key_hat), parts
        )
        query_back = both(
            through_norm, query_rate, query_scaled, query_hat, (dots[0][0] / D, dots[1][0] / D)
        )
        key_back = both(
            through_norm, key_rate, key_scaled, key_hat, (dots[0][1] / D, dots[1][1] / D)
        )
        back = both(
            lambda *parts: jnp.concatenate(parts, axis=1).astype(LOW),
            query_back,
            key_back,
            value_back,
        )
        return back, parts, half_of_both(*gateup_parts), down_halves

    rows_in, ride_in = lax.optimization_barrier(
        (
            (attended_back_low, attend_part),
            grad_gateup,
        )
    )
    gateup_parts = (give_near(ride_in[0]), slice_far(ride_in[1]))
    projected_back_low, parts, gateup_half, down_halves = lax.optimization_barrier(
        attend_whole_back(rows_in, gateup_parts, down_grads)
    )
    grad_heads = [weight_grad(projected_back_low, rows) for rows in halves(whole)]
    heads_parts = (give_near(grad_heads[0]), slice_far(grad_heads[1]))

    first, second = after(grad_heads, projected_back_low)
    arrived = to_core(contract(second, heads, 1, 1).astype(LOW))
    first, arrived = lax.optimization_barrier((contract(first, heads, 1, 1).astype(LOW), arrived))
    mine = add_low(first, arrived)
    attended_back, down_halves, parts = after(mine, (attended_back, down_halves, parts))
    grad_merge = [
        contract(mixed_whole, rows, 0, 0).astype(LOW)
        for rows in (attended_back[:, :HALF], attended_back[:, HALF:])
    ]

    rows = by_slice(parts[:, :2])
    rows = jnp.moveaxis(rows, 1, 0).reshape(4, HALF)
    width = jnp.sum(parts[:, 2:], axis=0).reshape(2, 2, HALF)
    width = jnp.where(high == 0, width, width[:, ::-1]).reshape(4, HALF)
    gains = jnp.concatenate([rows, width, jnp.zeros((24, HALF), WIDE)], axis=0).astype(LOW)
    merge_near = jnp.concatenate([grad_merge[0], gains], axis=0)
    merge_far = jnp.concatenate([grad_merge[1], gains], axis=0)

    merge_parts = (give_near(merge_near), slice_far(merge_far))
    small_parts = both(lambda *parts: jnp.concatenate(parts, axis=0), heads_parts, merge_parts)
    small_parts, gateup_arrived = lax.optimization_barrier(
        (small_parts, to_sibling(gateup_half))
    )
    arrived, grad_down, small_half = lax.optimization_barrier(
        (
            exchange(mine),
            whole_of_half(*down_halves).astype(WIDE),
            half_of_both(*small_parts),
        )
    )
    tokens_back = jnp.sum(arrived.reshape(8, SUB, D).astype(WIDE), axis=0)
    small_arrived, grad_gateup, grad_tokens = lax.optimization_barrier(
        (
            to_sibling(small_half),
            spread_gateup(whole_of_half(gateup_half, gateup_arrived)),
            ungroup((hidden_back + tokens_back).astype(LOW)),
        )
    )
    small = whole_of_half(small_half, small_arrived)
    grad_heads = spread_heads(small)
    grad_merge = small[3 * HEAD_DIM : 4 * HEAD_DIM].astype(WIDE)
    gains = small[4 * HEAD_DIM : 4 * HEAD_DIM + 8].astype(WIDE).reshape(4, D)
    return (
        output,
        grad_tokens,
        grad_heads,
        grad_merge,
        grad_gateup,
        grad_down,
        gains[0],
        gains[1],
        gains[2],
        gains[3],
    )


def solution(mesh):
    fine = Mesh(mesh.devices.reshape(tuple(SIZES[name] for name in NAMES)), NAMES)
    dp, row, col = ("yl", "core"), ("xh", "xl", "z"), "yh"
    in_specs = (
        P(dp + row, col),
        P(col, None, row),
        P(row),
        P(row),
        P(row, col),
        P(col),
        P(col, None, row),
        P(row, col),
        P(col),
        P(dp + row, col),
    )
    out_specs = (
        P(dp + row, col),
        P(dp + row, col),
        P(col, None, row),
        P(row, col),
        P(col, None, row),
        P(row, col),
        P(),
        P(),
        P(),
        P(),
    )
    return jax.shard_map(local, mesh=fine, in_specs=in_specs, out_specs=out_specs, check_vma=False)
```

```python
import itertools

import jax
import jax.numpy as jnp
from jax import lax
from jax.experimental import pallas as pl
from jax.experimental.pallas import tpu as pltpu
from jax.sharding import Mesh
from jax.sharding import PartitionSpec as P

D = 2048
HEAD_DIM = 128
SEQ_LEN = 1024
HALF = 1024
SUB = 64
EPSILON = 1e-06
THETA = 500000.0
NEGATIVE = -1e30

LOW = jnp.bfloat16
WIDE = jnp.float32

NAMES = ("yl", "core", "xh", "xl", "z", "yh")
SIZES = {"yl": 2, "core": 2, "xh": 2, "xl": 2, "z": 4, "yh": 2}


def contract(left, right, left_dim, right_dim):
    return lax.dot_general(
        left, right, (((left_dim,), (right_dim,)), ((), ())), preferred_element_type=WIDE
    )


def pairs_of(axes, target):
    sizes = [SIZES[name] for name in axes]

    def flat(place):
        index = 0
        for value, size in zip(place, sizes):
            index = index * size + value
        return index

    return [
        (flat(place), flat(target(*place)))
        for place in itertools.product(*[range(size) for size in sizes])
    ]


def move(value, axes, target):
    return lax.ppermute(value, axes, pairs_of(axes, target))


def to_core(value):
    return move(value, ("core",), lambda c: (1 - c,))


def to_sibling(value):
    return move(value, ("yl",), lambda a: (1 - a,))


def slice_near(value):
    return move(
        value,
        ("core", "xh", "xl"),
        lambda c, a, b: (c, 1 - a, 1 - b) if c == a else (1 - c, a, b),
    )


def give_near(value):
    return move(
        value,
        ("core", "xh", "xl"),
        lambda c, a, b: (1 - c, a, b) if c == a else (c, 1 - a, 1 - b),
    )


def slice_far(value):
    return move(
        value,
        ("yl", "core", "xh", "xl", "yh"),
        lambda l, c, a, b, h: (1 - l, c, a, b, 1 - h)
        if c == a
        else (1 - l, 1 - c, 1 - a, 1 - b, 1 - h),
    )


def after(value, arrays):
    return lax.optimization_barrier((value, arrays))[1]


def beside(function, value, rides, work=()):
    value, arrays = lax.optimization_barrier((value, tuple(array for _, array in rides)))
    moved = tuple(ride(array) for (ride, _), array in zip(rides, arrays))
    return lax.optimization_barrier((function(value), moved, work))


def exchange(rows):
    return lax.all_to_all(rows, ("xl", "z"), 0, 0, tiled=True)


def scatter_parts(function, rides=()):
    arrived = to_core(function(1))
    own, arrived = lax.optimization_barrier((function(0), arrived))
    arrived, moved, _ = beside(exchange, add_low(own, arrived), rides)
    return arrived, moved


def by_core(first, second):
    own_first = lax.axis_index("core") == 0
    return jnp.where(own_first, first, second), jnp.where(own_first, second, first)


def group_copies(rows):
    copies = jnp.broadcast_to(rows[None], (16,) + rows.shape).reshape(-1, 128)
    arrived = lax.all_to_all(copies, ("core", "xl", "z"), 0, 0, tiled=True)
    return arrived.reshape((16,) + rows.shape)


def group_sums(own, other, more=None):
    whole = jnp.concatenate(by_core(own, other), axis=0).reshape(16, 128)
    if more is not None:
        whole = jnp.concatenate([whole, more], axis=0)
    arrived = group_copies(whole)
    total = jnp.sum(arrived[:, :16], axis=0).reshape(2, 2, 512)
    return by_core(total[0], total[1]), arrived[:, 16:]


def by_slice(blocks):
    view = blocks.reshape((2, 2, 4) + blocks.shape[1:])
    straight = jnp.arange(2) == lax.axis_index("xh")
    straight = straight.reshape((2,) + (1,) * (view.ndim - 2))
    first = jnp.where(straight, view[:, 0], view[:, 1])
    second = jnp.where(straight, view[:, 1], view[:, 0])
    return jnp.stack([first, second], axis=1).reshape(blocks.shape)


def to_owners(own, other):
    blocks = jnp.concatenate(by_core(own, other), axis=0)
    arrived = lax.all_to_all(blocks, ("core", "xl", "z"), 0, 0, tiled=True)
    return jnp.swapaxes(arrived.reshape(16, SUB, HEAD_DIM), 0, 1).reshape(SUB, D)


def to_heads(rows):
    blocks = jnp.swapaxes(rows.reshape(SUB, 16, HEAD_DIM), 0, 1).reshape(16 * SUB, HEAD_DIM)
    return lax.all_to_all(blocks, ("core", "xl", "z"), 0, 0, tiled=True)


def both(function, *pairs):
    return tuple(function(*items) for items in zip(*pairs))


def halves(pair):
    return tuple(rows[:, :HALF] for rows in pair), tuple(rows[:, HALF:] for rows in pair)


def add_low(first, *others):
    total = first.astype(WIDE)
    for other in others:
        total = total + other.astype(WIDE)
    return total.astype(LOW)


def regroup(block):
    core = lax.axis_index("core")
    high = lax.axis_index("yh")
    lower, upper = block[:SUB], block[SUB:]
    parts = []
    for j in (0, 1):
        piece = jnp.where((high ^ j) == 0, lower, upper)
        parts.append(move(piece, ("core", "yh"), lambda c, h: (h ^ j, c)))
    same = core == high
    return jnp.concatenate(
        [jnp.where(same, parts[0], parts[1]), jnp.where(same, parts[1], parts[0])], axis=1
    )


def ungroup(block):
    core = lax.axis_index("core")
    high = lax.axis_index("yh")
    near, far = block[:, :HALF], block[:, HALF:]
    parts = []
    for j in (0, 1):
        piece = jnp.where((core ^ j) == high, near, far)
        parts.append(move(piece, ("core", "yh"), lambda c, h: (h, c ^ j)))
    first = high == 0
    return jnp.concatenate(
        [jnp.where(first, parts[0], parts[1]), jnp.where(first, parts[1], parts[0])], axis=0
    )


def half_of_both(arrived_near, arrived_far):
    part = arrived_near.astype(WIDE) + arrived_far.astype(WIDE)
    rows = part.shape[0] // 2
    core = lax.axis_index("core")
    lower, upper = part[:rows], part[rows:]
    keep = jnp.where(core == 0, lower, upper)
    give = jnp.where(core == 0, upper, lower).astype(LOW)
    return (keep + to_core(give).astype(WIDE)).astype(LOW)


def halves_of_sibling(parts):
    half = half_of_both(*parts)
    return half, to_sibling(half)


def whole_of_half(half, arrived):
    core = lax.axis_index("core")
    half = add_low(half, arrived)
    other = to_core(half)
    return jnp.concatenate(
        [jnp.where(core == 0, half, other), jnp.where(core == 0, other, half)], axis=0
    )


def rope_tables(place):
    pairs = HEAD_DIM // 2
    freq = THETA ** (-(jnp.arange(pairs, dtype=WIDE) * (2.0 / HEAD_DIM)))
    angle = place.astype(WIDE)[:, None] * freq[None, :]
    cosine = jnp.concatenate([jnp.cos(angle), jnp.cos(angle)], axis=1)
    sine = jnp.concatenate([jnp.sin(angle), jnp.sin(angle)], axis=1)
    return (cosine, sine)


def rotate(values, cosine, sine):
    pairs = HEAD_DIM // 2
    turned = jnp.concatenate([-values[:, pairs:], values[:, :pairs]], axis=1)
    return values * cosine + turned * sine


def rotate_back(grad, cosine, sine):
    pairs = HEAD_DIM // 2
    scaled = grad * sine
    turned = jnp.concatenate([scaled[:, pairs:], -scaled[:, :pairs]], axis=1)
    return grad * cosine + turned


ROWS = 256
SCALE = HEAD_DIM ** (-0.5)


def places_of(index, core):
    block, row = (index % 512) // SUB, index % SUB
    return block * 128 + jnp.where(index < 512, core, 1 - core) * SUB + row


def block_scores(core_ref, query, key):
    first = pl.program_id(0) * ROWS
    query_index = first + lax.broadcasted_iota(jnp.int32, (ROWS, 1), 0)
    key_index = lax.broadcasted_iota(jnp.int32, (1, SEQ_LEN), 1)
    core = core_ref[0]
    allowed = places_of(key_index, core) <= places_of(query_index, core)
    return jnp.where(allowed, contract(query, key, 1, 1) * SCALE, NEGATIVE)


def attend_kernel(core_ref, query_ref, key_ref, value_ref, mixed_ref, total_ref):
    scores = block_scores(core_ref, query_ref[...], key_ref[...])
    top = jnp.max(scores, axis=1, keepdims=True)
    shifted = jnp.exp(scores - top)
    total = jnp.sum(shifted, axis=1, keepdims=True)
    probs_low = (shifted * (1.0 / total)).astype(LOW)
    mixed_ref[...] = contract(probs_low, value_ref[...], 1, 0).astype(LOW)
    total_ref[...] = jnp.broadcast_to(top + jnp.log(total), total_ref.shape)


def attend_back_kernel(
    core_ref,
    query_ref,
    key_ref,
    value_ref,
    total_ref,
    mixed_back_ref,
    query_out,
    key_out,
    value_out,
):
    query, key, mixed_back = query_ref[...], key_ref[...], mixed_back_ref[...]
    probs = jnp.exp(block_scores(core_ref, query, key) - total_ref[...][:, :1])
    probs_back = contract(mixed_back, value_ref[...], 1, 1)
    row_dot = jnp.sum(probs_back * probs, axis=1, keepdims=True)
    scores_back = (probs * (probs_back - row_dot)).astype(LOW)
    query_out[...] = contract(scores_back, key, 1, 0) * SCALE
    key_part = contract(scores_back, query, 0, 0) * SCALE
    value_part = contract(probs.astype(LOW), mixed_back, 0, 0)

    @pl.when(pl.program_id(0) == 0)
    def _():
        key_out[...] = key_part
        value_out[...] = value_part

    @pl.when(pl.program_id(0) > 0)
    def _():
        key_out[...] += key_part
        value_out[...] += value_part


def row_spec():
    return pl.BlockSpec((ROWS, HEAD_DIM), lambda i: (i, 0))


def whole_spec():
    return pl.BlockSpec((SEQ_LEN, HEAD_DIM), lambda i: (0, 0))


def core_spec():
    return pl.BlockSpec(memory_space=pltpu.SMEM)


def head_call(kernel, in_specs, out_specs, out_types):
    return pl.pallas_call(
        kernel,
        grid=(SEQ_LEN // ROWS,),
        in_specs=in_specs,
        out_specs=out_specs,
        out_shape=[jax.ShapeDtypeStruct((SEQ_LEN, HEAD_DIM), kind) for kind in out_types],
        compiler_params=pltpu.CompilerParams(vmem_limit_bytes=32 * 1024 * 1024),
        cost_estimate=pl.CostEstimate(flops=0, bytes_accessed=0, transcendentals=0),
    )


def attend(core, query, key, value):
    return head_call(
        attend_kernel,
        [core_spec(), row_spec(), whole_spec(), whole_spec()],
        [row_spec(), row_spec()],
        [LOW, WIDE],
    )(core, query, key, value)


def attend_back(core, query, key, value, total, mixed_back):
    return head_call(
        attend_back_kernel,
        [core_spec(), row_spec(), whole_spec(), whole_spec(), row_spec(), row_spec()],
        [row_spec(), whole_spec(), whole_spec()],
        [WIDE, WIDE, WIDE],
    )(core, query, key, value, total, mixed_back)


def spread_kernel(rows_ref, heads_ref):
    for i in range(3):
        part = rows_ref[i * HEAD_DIM : (i + 1) * HEAD_DIM, :]
        heads_ref[:, i, :] = jnp.transpose(part.astype(WIDE))


def spread_heads(rows):
    return pl.pallas_call(
        spread_kernel,
        grid=(2,),
        in_specs=[pl.BlockSpec((3 * HEAD_DIM, 512), lambda i: (0, i))],
        out_specs=pl.BlockSpec((512, 3, HEAD_DIM), lambda i: (i, 0, 0)),
        out_shape=jax.ShapeDtypeStruct((HALF, 3, HEAD_DIM), WIDE),
        compiler_params=pltpu.CompilerParams(vmem_limit_bytes=32 * 1024 * 1024),
    )(rows)


def spread_gateup_kernel(rows_ref, gateup_ref):
    for i in range(2):
        gateup_ref[:, i, :] = rows_ref[:, i * 512 : (i + 1) * 512].astype(WIDE)


def spread_gateup(rows):
    return pl.pallas_call(
        spread_gateup_kernel,
        grid=(4,),
        in_specs=[pl.BlockSpec((256, HALF), lambda i: (i, 0))],
        out_specs=pl.BlockSpec((256, 2, 512), lambda i: (i, 0, 0)),
        out_shape=jax.ShapeDtypeStruct((HALF, 2, 512), WIDE),
        compiler_params=pltpu.CompilerParams(vmem_limit_bytes=32 * 1024 * 1024),
    )(rows)


LIMIT = pltpu.CompilerParams(vmem_limit_bytes=40 * 1024 * 1024)


def estimate(flops, moved):
    return pl.CostEstimate(flops=flops, bytes_accessed=moved, transcendentals=0)


def feed_kernel(rows_ref, gate_w_ref, upper_w_ref, gate_ref, upper_ref, act_ref):
    rows = rows_ref[...]
    gate = contract(rows, gate_w_ref[...], 1, 0)
    upper = contract(rows, upper_w_ref[...], 1, 0)
    gate_ref[...] = gate
    upper_ref[...] = upper
    act_ref[...] = (gate * jax.nn.sigmoid(gate) * upper).astype(LOW)


def feed(rows, weight):
    part = pl.BlockSpec((512, 256), lambda i: (0, i))
    wide = jax.ShapeDtypeStruct((512, 512), WIDE)
    return pl.pallas_call(
        feed_kernel,
        grid=(2,),
        in_specs=[
            pl.BlockSpec((512, D), lambda i: (0, 0)),
            pl.BlockSpec((D, 256), lambda i: (0, i)),
            pl.BlockSpec((D, 256), lambda i: (0, i + 2)),
        ],
        out_specs=[part, part, part],
        out_shape=[wide, wide, jax.ShapeDtypeStruct((512, 512), LOW)],
        compiler_params=LIMIT,
        cost_estimate=estimate(2 * 512 * D * 1024, 8 * 1024 * 1024),
    )(rows, weight, weight)


def feed_out_kernel(act_ref, near_ref, far_ref, out_ref):
    act = act_ref[...]
    out_ref[:, :HALF] = contract(act, near_ref[...], 1, 0).astype(LOW)
    out_ref[:, HALF:] = contract(act, far_ref[...], 1, 0).astype(LOW)


def feed_out(act, near, far):
    whole = pl.BlockSpec((512, HALF), lambda i: (0, 0))
    return pl.pallas_call(
        feed_out_kernel,
        grid=(2,),
        in_specs=[pl.BlockSpec((256, 512), lambda i: (i, 0)), whole, whole],
        out_specs=pl.BlockSpec((256, D), lambda i: (i, 0)),
        out_shape=jax.ShapeDtypeStruct((512, D), LOW),
        compiler_params=LIMIT,
        cost_estimate=estimate(2 * 512 * 512 * D, 5 * 1024 * 1024),
    )(act, near, far)


def feed_back_kernel(rows_ref, near_ref, far_ref, gate_ref, upper_ref, out_ref):
    act_back = contract(rows_ref[:, :HALF], near_ref[...], 1, 1) + contract(
        rows_ref[:, HALF:], far_ref[...], 1, 1
    )
    gate, upper = gate_ref[...], upper_ref[...]
    sigmoid = jax.nn.sigmoid(gate)
    gate_back = act_back * upper * sigmoid * (1.0 + gate * (1.0 - sigmoid))
    out_ref[:, :512] = gate_back.astype(LOW)
    out_ref[:, 512:] = (act_back * (gate * sigmoid)).astype(LOW)


def feed_back(rows, near, far, gate, upper):
    whole = pl.BlockSpec((512, HALF), lambda i: (0, 0))
    part = pl.BlockSpec((256, 512), lambda i: (i, 0))
    return pl.pallas_call(
        feed_back_kernel,
        grid=(2,),
        in_specs=[pl.BlockSpec((256, D), lambda i: (i, 0)), whole, whole, part, part],
        out_specs=pl.BlockSpec((256, HALF), lambda i: (i, 0)),
        out_shape=jax.ShapeDtypeStruct((512, HALF), LOW),
        compiler_params=LIMIT,
        cost_estimate=estimate(2 * 512 * 512 * D, 7 * 1024 * 1024),
    )(rows, near, far, gate, upper)


def dense_kernel(arrived_ref, hidden_ref, cotangent_ref, scale_ref, copies_ref, out_ref, part_ref):
    dense = jnp.sum(arrived_ref[...].astype(WIDE), axis=0)
    rate = lax.rsqrt(jnp.mean(dense * dense, axis=1, keepdims=True) + EPSILON)
    hat = dense * rate
    scale = scale_ref[...]
    out_ref[...] = (hidden_ref[...] + hat * scale).astype(LOW)
    cotangent = cotangent_ref[...].astype(WIDE)
    part_ref[...] = jnp.sum(cotangent * hat, axis=0, keepdims=True)
    scaled = cotangent * scale
    dot = jnp.mean(scaled * hat, axis=1, keepdims=True)
    back = (rate * (scaled - hat * dot)).astype(LOW)
    for i in range(8):
        copies_ref[i * SUB : (i + 1) * SUB, :] = back


def dense_step(arrived, hidden, cotangent, scale):
    return pl.pallas_call(
        dense_kernel,
        out_shape=[
            jax.ShapeDtypeStruct((8 * SUB, D), LOW),
            jax.ShapeDtypeStruct((SUB, D), LOW),
            jax.ShapeDtypeStruct((1, D), WIDE),
        ],
        compiler_params=LIMIT,
        cost_estimate=estimate(20 * SUB * D, 6 * 1024 * 1024),
    )(arrived.reshape(8, SUB, D), hidden, cotangent, scale[None])


def hidden_kernel(arrived_ref, cotangent_ref, hat_ref, rate_ref, scale_ref, out_ref, low_ref, part_ref):
    hidden_back = cotangent_ref[...].astype(WIDE) + jnp.sum(arrived_ref[...].astype(WIDE), axis=0)
    hat = hat_ref[...]
    out_ref[...] = hidden_back
    part_ref[...] = jnp.sum(hidden_back * hat, axis=0, keepdims=True)
    scaled = hidden_back * scale_ref[...]
    dot = jnp.mean(scaled * hat, axis=1, keepdims=True)
    low_ref[...] = (rate_ref[...] * (scaled - hat * dot)).astype(LOW)


def hidden_step(arrived, cotangent, hat, rate, scale):
    return pl.pallas_call(
        hidden_kernel,
        out_shape=[
            jax.ShapeDtypeStruct((SUB, D), WIDE),
            jax.ShapeDtypeStruct((SUB, D), LOW),
            jax.ShapeDtypeStruct((1, D), WIDE),
        ],
        compiler_params=LIMIT,
        cost_estimate=estimate(20 * SUB * D, 4 * 1024 * 1024),
    )(arrived.reshape(8, SUB, D), cotangent, hat, rate, scale[None])


def local(
    tokens,
    w_heads,
    query_scale,
    key_scale,
    w_merge,
    attend_scale,
    w_gateup,
    w_down,
    dense_scale,
    cotangent,
):
    core = lax.axis_index("core")
    xh = lax.axis_index("xh")
    xl = lax.axis_index("xl")
    z = lax.axis_index("z")
    high = lax.axis_index("yh")

    shard = regroup(tokens)
    heads_in = w_heads.reshape(HALF, 3 * HEAD_DIM)
    gateup_in = w_gateup.reshape(HALF, 2 * 512)

    index = jnp.arange(512, dtype=jnp.int32)
    place = index // SUB * 128 + index % SUB
    places = (place + core * SUB, place + (1 - core) * SUB)
    tables = both(rope_tables, places)
    core_in = core.astype(jnp.int32)[None]

    copies = jnp.broadcast_to(shard[None], (8,) + shard.shape).reshape(8 * SUB, D)
    merge_parts = (slice_near(w_merge), slice_far(w_merge))
    own, moved, (tables, gateup_in, merge) = beside(
        exchange,
        copies,
        (
            (slice_near, heads_in),
            (slice_far, heads_in),
        ),
        (tables, gateup_in, jnp.concatenate(merge_parts, axis=1)),
    )
    head_scales, width_scales = after(
        own, (jnp.stack([query_scale, key_scale]), jnp.stack([attend_scale, dense_scale]))
    )
    query_scale, key_scale = slice_near(head_scales)
    attend_scale, dense_scale = jnp.concatenate(
        [width_scales, move(width_scales, ("yl", "yh"), lambda l, h: (1 - l, 1 - h))], axis=1
    )
    heads = jnp.concatenate(moved, axis=0)
    merge = lax.all_gather(merge, ("core", "xl", "z"), axis=0, tiled=True)

    def squares(query, key):
        return jnp.stack([jnp.sum(query * query, axis=1), jnp.sum(key * key, axis=1)])

    def attend_whole(own):
        first, other = lax.optimization_barrier((contract(own, heads, 1, 0), to_core(own)))
        projected = (first, contract(other, heads, 1, 0))
        query_raw = both(lambda rows: rows[:, :HEAD_DIM], projected)
        key_raw = both(lambda rows: rows[:, HEAD_DIM : 2 * HEAD_DIM], projected)
        value_low = jnp.concatenate(
            both(lambda rows: rows[:, 2 * HEAD_DIM :].astype(LOW), projected), axis=0
        )
        powers, _ = group_sums(*both(squares, query_raw, key_raw))
        rates = both(lambda rows: lax.rsqrt(rows / D + EPSILON), powers)
        query_rate = both(lambda rows: rows[0][:, None], rates)
        key_rate = both(lambda rows: rows[1][:, None], rates)
        query_hat = both(lambda raw, rate: raw * rate, query_raw, query_rate)
        key_hat = both(lambda raw, rate: raw * rate, key_raw, key_rate)
        query_low = jnp.concatenate(
            both(
                lambda hat, table: rotate(hat * query_scale, *table).astype(LOW), query_hat, tables
            ),
            axis=0,
        )
        key_low = jnp.concatenate(
            both(lambda hat, table: rotate(hat * key_scale, *table).astype(LOW), key_hat, tables),
            axis=0,
        )

        mixed_low, log_total = attend(core_in, query_low, key_low, value_low)
        attended = contract(to_owners(mixed_low[:512], mixed_low[512:]), merge, 1, 0)
        return (
            (own, other),
            (query_rate, key_rate, query_hat, key_hat),
            (query_low, key_low, value_low),
            mixed_low,
            log_total,
            attended,
        )

    (whole, norms, lows, mixed_low, log_total, attended), gateup_parts, _ = beside(
        attend_whole, own, ((slice_near, gateup_in), (slice_far, gateup_in))
    )
    query_rate, key_rate, query_hat, key_hat = norms
    query_low, key_low, value_low = lows
    attend_rate = lax.rsqrt(jnp.mean(attended * attended, axis=1, keepdims=True) + EPSILON)
    attend_hat = attended * attend_rate
    hidden = shard.astype(WIDE) + attend_hat * attend_scale

    copies = jnp.broadcast_to(hidden.astype(LOW)[None], (8, SUB, D)).reshape(8 * SUB, D)
    own, down_parts, gateup_w = beside(
        exchange,
        copies,
        ((slice_near, w_down), (slice_far, w_down)),
        jnp.concatenate(gateup_parts, axis=0),
    )

    first, other = lax.optimization_barrier((feed(own, gateup_w), to_core(own)))
    fed = (first, feed(other, gateup_w))
    hidden_whole = (own, other)
    act_low = both(lambda parts: parts[2], fed)
    arrived, (grad_out,) = scatter_parts(
        lambda i: feed_out(act_low[i], *down_parts), ((regroup, cotangent),)
    )
    copies, output, dense_part = dense_step(arrived, hidden, grad_out, dense_scale)

    own, (output,), _ = beside(exchange, copies, ((ungroup, output),))

    def back_through(i, rows):
        return feed_back(rows, *down_parts, fed[i][0], fed[i][1])

    first, other = lax.optimization_barrier((back_through(0, own), to_core(own)))
    dense_back = (own, other)
    gateup_back_low = (first, back_through(1, other))

    def weight_grad(left, right):
        return (contract(left[0], right[0], 0, 0) + contract(left[1], right[1], 0, 0)).astype(LOW)

    grad_down = [weight_grad(act_low, rows) for rows in halves(dense_back)]
    arrived = to_core(contract(gateup_back_low[1], gateup_w, 1, 1).astype(LOW))
    first, arrived = lax.optimization_barrier(
        (contract(gateup_back_low[0], gateup_w, 1, 1).astype(LOW), arrived)
    )
    mine, *grad_down = lax.optimization_barrier((add_low(first, arrived), *grad_down))
    down_grads = (give_near(grad_down[0]), slice_far(grad_down[1]))
    back_in = after(mine, gateup_back_low)
    grad_gateup = tuple(weight_grad(rows, back_in) for rows in halves(hidden_whole))
    gateup_parts = (give_near(grad_gateup[0]), slice_far(grad_gateup[1]))
    arrived = exchange(mine)
    hidden_back, attended_back_low, attend_part = hidden_step(
        arrived, grad_out, attend_hat, attend_rate, attend_scale
    )
    attended_back = lax.all_gather(attended_back_low, ("core", "xl", "z"), axis=0, tiled=True)
    mixed_whole = jnp.concatenate(by_core(mixed_low[:512], mixed_low[512:]), axis=0)

    def products(query, query_hat, key, key_hat):
        return jnp.stack([jnp.sum(query * query_hat, axis=1), jnp.sum(key * key_hat, axis=1)])

    def through_norm(rate, scaled, hat, dot):
        return rate * (scaled - hat * dot[:, None])

    def column_sum(first, second):
        return sum(both(lambda a, b: jnp.sum(a * b, axis=0), first, second))

    def attend_whole_back(rows, gateup_parts, down_grads):
        attended_back_low, attend_part = rows
        mixed_back, down_grads = lax.optimization_barrier(
            (contract(attended_back_low, merge, 1, 1), down_grads)
        )
        down_half = half_of_both(*down_grads)
        mixed_back_low = to_heads(mixed_back.astype(LOW))
        mixed_back_low = jnp.concatenate(by_core(mixed_back_low[:512], mixed_back_low[512:]))
        (query_turned, key_turned, value_back), gateup_parts = lax.optimization_barrier(
            (
                attend_back(core_in, query_low, key_low, value_low, log_total, mixed_back_low),
                gateup_parts,
            )
        )
        query_norm_back = both(
            lambda rows, table: rotate_back(rows, *table),
            (query_turned[:512], query_turned[512:]),
            tables,
        )
        value_back = (value_back[:512], value_back[512:])
        key_norm_back = both(
            lambda rows, table: rotate_back(rows, *table),
            (key_turned[:512], key_turned[512:]),
            tables,
        )
        query_scaled = both(lambda rows: rows * query_scale, query_norm_back)
        key_scaled = both(lambda rows: rows * key_scale, key_norm_back)
        parts = jnp.concatenate(
            [
                column_sum(query_norm_back, query_hat)[None],
                column_sum(key_norm_back, key_hat)[None],
                attend_part.reshape(16, 128),
                dense_part.reshape(16, 128),
            ],
            axis=0,
        )
        dots, parts = group_sums(
            *both(products, query_scaled, query_hat, key_scaled, key_hat), parts
        )
        query_back = both(
            through_norm, query_rate, query_scaled, query_hat, (dots[0][0] / D, dots[1][0] / D)
        )
        key_back = both(
            through_norm, key_rate, key_scaled, key_hat, (dots[0][1] / D, dots[1][1] / D)
        )
        back = both(
            lambda *parts: jnp.concatenate(parts, axis=1).astype(LOW),
            query_back,
            key_back,
            value_back,
        )
        return back, parts, half_of_both(*gateup_parts), down_half

    projected_back_low, parts, gateup_half, down_half = lax.optimization_barrier(
        attend_whole_back((attended_back_low, attend_part), gateup_parts, down_grads)
    )
    grad_heads = [weight_grad(projected_back_low, rows) for rows in halves(whole)]
    heads_parts = (give_near(grad_heads[0]), slice_far(grad_heads[1]))

    first, second = after(grad_heads, projected_back_low)
    arrived = to_core(contract(second, heads, 1, 1).astype(LOW))
    first, arrived = lax.optimization_barrier((contract(first, heads, 1, 1).astype(LOW), arrived))
    mine = add_low(first, arrived)
    attended_back, parts = after(mine, (attended_back, parts))
    down_arrived = to_sibling(down_half)
    grad_merge = [
        contract(mixed_whole, rows, 0, 0).astype(LOW)
        for rows in (attended_back[:, :HALF], attended_back[:, HALF:])
    ]

    rows = by_slice(parts[:, :2])
    rows = jnp.moveaxis(rows, 1, 0).reshape(4, HALF)
    width = jnp.sum(parts[:, 2:], axis=0).reshape(2, 2, HALF)
    width = jnp.where(high == 0, width, width[:, ::-1]).reshape(4, HALF)
    gains = jnp.concatenate([rows, width, jnp.zeros((24, HALF), WIDE)], axis=0).astype(LOW)
    merge_near = jnp.concatenate([grad_merge[0], gains], axis=0)
    merge_far = jnp.concatenate([grad_merge[1], gains], axis=0)

    merge_parts = (give_near(merge_near), slice_far(merge_far))
    small_parts = both(lambda *parts: jnp.concatenate(parts, axis=0), heads_parts, merge_parts)
    small_parts, gateup_arrived = lax.optimization_barrier(
        (small_parts, to_sibling(gateup_half))
    )
    arrived, grad_down, small_half = lax.optimization_barrier(
        (
            exchange(mine),
            whole_of_half(down_half, down_arrived).astype(WIDE),
            half_of_both(*small_parts),
        )
    )
    tokens_back = jnp.sum(arrived.reshape(8, SUB, D).astype(WIDE), axis=0)
    small_arrived, grad_gateup, grad_tokens = lax.optimization_barrier(
        (
            to_sibling(small_half),
            spread_gateup(whole_of_half(gateup_half, gateup_arrived)),
            ungroup((hidden_back + tokens_back).astype(LOW)),
        )
    )
    small = whole_of_half(small_half, small_arrived)
    grad_heads = spread_heads(small)
    grad_merge = small[3 * HEAD_DIM : 4 * HEAD_DIM].astype(WIDE)
    gains = small[4 * HEAD_DIM : 4 * HEAD_DIM + 8].astype(WIDE).reshape(4, D)
    return (
        output,
        grad_tokens,
        grad_heads,
        grad_merge,
        grad_gateup,
        grad_down,
        gains[0],
        gains[1],
        gains[2],
        gains[3],
    )


def solution(mesh):
    fine = Mesh(mesh.devices.reshape(tuple(SIZES[name] for name in NAMES)), NAMES)
    dp, row, col = ("yl", "core"), ("xh", "xl", "z"), "yh"
    in_specs = (
        P(dp + row, col),
        P(col, None, row),
        P(row),
        P(row),
        P(row, col),
        P(col),
        P(col, None, row),
        P(row, col),
        P(col),
        P(dp + row, col),
    )
    out_specs = (
        P(dp + row, col),
        P(dp + row, col),
        P(col, None, row),
        P(row, col),
        P(col, None, row),
        P(row, col),
        P(),
        P(),
        P(),
        P(),
    )
    return jax.shard_map(local, mesh=fine, in_specs=in_specs, out_specs=out_specs, check_vma=False)
```
